256 devices in a mesh: spatial: 16 (over z, core), head: 4 (over x), dp: 4 (over y).
Axes of the slice: x: 4, y: 4, z: 8, core: 2. Of those that a mesh axis runs over, the one named last changes fastest.
Arguments:
- tokens: bfloat16 [4, 4096, 1024], P('dp', 'spatial'), may hold values from -6 to 6
- neighbours: int32 [4, 64, 27], P('dp', 'spatial'), may hold values from -1 to 63, as said below
- counts: int32 [4, 64], P('dp'), may hold values from 1 to 64, as said below
- w_qkv: bfloat16 [3, 1024, 1024], P(None, None, 'head'), may hold values from -0.1875 to 0.1875
- w_out: bfloat16 [1024, 1024], P('head'), may hold values from -0.1875 to 0.1875
- cotangent: bfloat16 [4, 4096, 1024], P('dp', 'spatial'), may hold values from -6 to 6
Outputs:
- layer_out: bfloat16 [4, 4096, 1024], P('dp', 'spatial', 'head')
- grad_tokens: bfloat16 [4, 4096, 1024], P('dp', 'spatial', 'head')
- grad_qkv: float32 [3, 1024, 1024], P(None, None, 'head')
- grad_out: float32 [1024, 1024], P('head')
The draws below stay inside these ranges and needn't reach their ends.
Inputs may be any that keep to these rules, and one draw needn't show every extreme that they name: neighbours[s, b, 0] = b; every other entry is -1 (an empty slot) or a block c with 0 < |c - b| <= 4; no block appears twice in a row; in every scene some block lists the block exactly 4 after it. `counts`: the occupied tokens of a block fill its first slots.
All inputs are finite; a program needn't handle non-finite values.
Results may differ from the reference program's by a relative error of at most 0.012.
The reference program's roundings to bfloat16 on the way (of `upstream`, `probs_low`, `attended`, `dscore`, `query_grad`, `key_grad` and `value_grad`) count: a program that leaves them out, or rounds other values in their place, can miss the bound.
Values may be sent and summed in bfloat16 or wider, within the bound.
No kernel may reach another device: no remote copies, remote signals or barrier semaphores. Data moves between devices by JAX's collectives and lax.ppermute only.
A program may use at most 192 MiB of HBM per device.

```python
import jax
import jax.numpy as jnp
from jax import lax

D = 1024
HEADS = 16
HD = 64
BLOCK = 64
NBR = 27
HD_ALL = 1024
BLK_DEV = 4
NBLK = 64
TOKENS = 4096
SCENES = 4


def draw_neighbours(key, part):
    key = jax.random.fold_in(key, 11)
    first_key, second_key = jax.random.split(key, 2)
    base = jnp.arange(NBLK, dtype=jnp.int32)[None, :, None]
    offset = jax.random.randint(first_key, (SCENES, NBLK, NBR), -BLK_DEV, BLK_DEV + 1)
    offset = offset.at[:, :, 0].set(0)
    offset = offset.at[:, 0, 1].set(BLK_DEV)
    offset = offset.at[:, 0, 2].set(-1)
    listed = base + offset
    dropped = jax.random.randint(second_key, (SCENES, NBLK, NBR), 0, 10) < 3
    dropped = dropped.at[:, :, 0].set(False)
    dropped = dropped.at[:, 0, 1].set(False)
    outside = (listed < 0) | (listed >= NBLK)
    earlier = jnp.tril(jnp.ones((NBR, NBR), dtype=bool), -1)
    repeated = jnp.any((listed[..., :, None] == listed[..., None, :]) & earlier, axis=-1)
    listed = jnp.where(dropped | outside | repeated, -1, listed)
    return listed.astype(jnp.int32)


def draw_counts(key, part):
    key = jax.random.fold_in(key, 23)
    occupied = jax.random.randint(key, (SCENES, NBLK), 1, BLOCK + 1)
    occupied = occupied.at[:, 0].set(BLOCK)
    return occupied.astype(jnp.int32)


def level_of(stream_key, dims, cuts, low, largest):
    gain = 1.0
    for dim, parts in cuts:
        draws = jax.random.uniform(jax.random.fold_in(jax.random.fold_in(stream_key, 6), dim), (parts,), jnp.float32, low / len(cuts), largest / len(cuts))
        gain = gain * jnp.repeat(jnp.exp(draws), dims[dim] // parts).reshape((-1,) + (1,) * (len(dims) - 1 - dim))
    return gain


def bell_draw(own_key, dims, width, limit, cuts=(), kind=jnp.bfloat16):
    result = width * jax.random.normal(own_key, dims, jnp.float32)
    if cuts:
        result = result * level_of(own_key, dims, cuts, -0.22, 0.18)
    return jnp.clip(result, -limit, limit).astype(kind)


def setup_inputs(seed: int = 0) -> dict:
    keys = jax.random.split(jax.random.key(seed), 7)
    return {
        "tokens": bell_draw(keys[0], (SCENES, TOKENS, D), 1.0, 6.0, ((0, 4), (1, 16))),
        "neighbours": draw_neighbours(jax.random.fold_in(keys[6], 71), 0),
        "counts": draw_counts(jax.random.fold_in(keys[6], 71), 0),
        "w_qkv": bell_draw(keys[3], (3, D, HD_ALL), D ** -0.5, 0.1875, ((2, 4),)),
        "w_out": bell_draw(keys[4], (HD_ALL, D), HD_ALL ** -0.5, 0.1875, ((0, 4),)),
        "cotangent": bell_draw(keys[5], (SCENES, TOKENS, D), 1.0, 6.0, ((0, 4), (1, 16))),
    }


def scene_pass(scene_tokens, block_ids, occupied, w_qkv, w_out, scene_cot):
    factor = HD ** -0.5
    queries = jnp.dot(scene_tokens, w_qkv[0], preferred_element_type=jnp.float32).astype(jnp.bfloat16)
    keys_all = jnp.dot(scene_tokens, w_qkv[1], preferred_element_type=jnp.float32).astype(jnp.bfloat16)
    values_all = jnp.dot(scene_tokens, w_qkv[2], preferred_element_type=jnp.float32).astype(jnp.bfloat16)
    upstream = jnp.dot(scene_cot, w_out.T, preferred_element_type=jnp.float32).astype(jnp.bfloat16)
    q_blocks = queries.reshape(NBLK, BLOCK, HEADS, HD).astype(jnp.float32)
    k_blocks = keys_all.reshape(NBLK, BLOCK, HEADS, HD).astype(jnp.float32)
    v_blocks = values_all.reshape(NBLK, BLOCK, HEADS, HD).astype(jnp.float32)
    up_blocks = upstream.reshape(NBLK, BLOCK, HEADS, HD).astype(jnp.float32)
    slots = jnp.arange(BLOCK, dtype=jnp.int32)
    groups = jnp.arange(NBLK, dtype=jnp.int32).reshape(NBLK // BLK_DEV, BLK_DEV)

    def one_group(running, members):
        key_grad, value_grad = running
        listed = block_ids[members]
        clipped = jnp.maximum(listed, 0)
        usable = (listed >= 0)[:, :, None] & (slots[None, None, :] < occupied[clipped][:, :, None])
        usable = usable.reshape(BLK_DEV, NBR * BLOCK)
        near_keys = k_blocks[clipped].reshape(BLK_DEV, NBR * BLOCK, HEADS, HD)
        near_values = v_blocks[clipped].reshape(BLK_DEV, NBR * BLOCK, HEADS, HD)
        own_q = q_blocks[members]
        own_up = up_blocks[members]
        scores = jnp.einsum("gqhd,gkhd->ghqk", own_q, near_keys) * factor
        weights = jnp.where(usable[:, None, None, :], jnp.exp(scores), 0.0)
        probs = weights / jnp.sum(weights, axis=-1, keepdims=True)
        probs_low = lax.optimization_barrier(probs.astype(jnp.bfloat16)).astype(jnp.float32)
        attended = jnp.einsum("ghqk,gkhd->gqhd", probs_low, near_values).astype(jnp.bfloat16)
        dprob = jnp.einsum("gqhd,gkhd->ghqk", own_up, near_values)
        spread = jnp.sum(probs * dprob, axis=-1, keepdims=True)
        dscore = lax.optimization_barrier((probs * (dprob - spread) * factor).astype(jnp.bfloat16)).astype(jnp.float32)
        query_grad = jnp.einsum("ghqk,gkhd->gqhd", dscore, near_keys).astype(jnp.bfloat16)
        key_part = jnp.einsum("ghqk,gqhd->gkhd", dscore, own_q).reshape(BLK_DEV, NBR, BLOCK, HEADS, HD)
        value_part = jnp.einsum("ghqk,gqhd->gkhd", probs_low, own_up).reshape(BLK_DEV, NBR, BLOCK, HEADS, HD)
        key_grad = key_grad.at[clipped].add(key_part)
        value_grad = value_grad.at[clipped].add(value_part)
        return (key_grad, value_grad), (attended, query_grad)

    empty = jnp.zeros((NBLK, BLOCK, HEADS, HD), jnp.float32)
    (key_grad, value_grad), (attended, query_grad) = lax.scan(one_group, (empty, empty), groups)
    attended = attended.reshape(TOKENS, HD_ALL)
    query_grad = query_grad.reshape(TOKENS, HD_ALL)
    key_low = key_grad.reshape(TOKENS, HD_ALL).astype(jnp.bfloat16)
    value_low = value_grad.reshape(TOKENS, HD_ALL).astype(jnp.bfloat16)
    layer_out = (scene_tokens.astype(jnp.float32) + jnp.dot(attended, w_out, preferred_element_type=jnp.float32)).astype(jnp.bfloat16)
    inner = jnp.dot(query_grad, w_qkv[0].T, preferred_element_type=jnp.float32)
    inner = inner + jnp.dot(key_low, w_qkv[1].T, preferred_element_type=jnp.float32)
    inner = inner + jnp.dot(value_low, w_qkv[2].T, preferred_element_type=jnp.float32)
    grad_tokens = (scene_cot.astype(jnp.float32) + inner).astype(jnp.bfloat16)
    qkv_grad = jnp.stack([jnp.dot(scene_tokens.T, which, preferred_element_type=jnp.float32) for which in (query_grad, key_low, value_low)])
    out_grad = jnp.dot(attended.T, scene_cot, preferred_element_type=jnp.float32)
    return layer_out, grad_tokens, qkv_grad, out_grad


def reference(tokens, neighbours, counts, w_qkv, w_out, cotangent):
    outputs = []
    grads_in = []
    qkv_total = jnp.zeros((3, D, HD_ALL), jnp.float32)
    out_total = jnp.zeros((HD_ALL, D), jnp.float32)
    for scene in range(SCENES):
        layer_out, grad_tokens, qkv_grad, out_grad = scene_pass(tokens[scene], neighbours[scene], counts[scene], w_qkv, w_out, cotangent[scene])
        outputs.append(layer_out)
        grads_in.append(grad_tokens)
        qkv_total = qkv_total + qkv_grad
        out_total = out_total + out_grad
    return jnp.stack(outputs), jnp.stack(grads_in), qkv_total, out_total
```

```python
import functools

import jax
import jax.numpy as jnp
from jax import lax
from jax.experimental import pallas as pl
from jax.experimental.pallas import tpu as pltpu
from jax.sharding import PartitionSpec as P

HD = 64
BLOCK = 64
ROWS = 256
WIDTH = 256
D = 1024
REACH = 4
LOG2E = 1.4426950408889634
BF = jnp.bfloat16
F32 = jnp.float32
VMEM = pl.BlockSpec(memory_space=pltpu.VMEM)
SMEM = pl.BlockSpec(memory_space=pltpu.SMEM)


def call(kernel, outs, operands, flops, in_specs=None, scratch=(), vmem=24):
    moved = sum(a.size * a.dtype.itemsize for a in operands)
    moved += sum(o.size * o.dtype.itemsize for o in outs)
    return pl.pallas_call(
        kernel,
        out_shape=outs,
        in_specs=in_specs or [VMEM] * len(operands),
        out_specs=[VMEM] * len(outs),
        scratch_shapes=list(scratch),
        compiler_params=pltpu.CompilerParams(vmem_limit_bytes=vmem * 2**20),
        cost_estimate=pl.CostEstimate(flops=flops, bytes_accessed=moved, transcendentals=0),
    )(*operands)


def shape(dims, kind):
    return jax.ShapeDtypeStruct(dims, kind)


def nn(a, b):
    return lax.dot_general(a, b, (((1,), (0,)), ((), ())), preferred_element_type=F32)


def nt(a, b):
    return lax.dot_general(a, b, (((1,), (1,)), ((), ())), preferred_element_type=F32)


def tn(a, b):
    return lax.dot_general(a, b, (((0,), (0,)), ((), ())), preferred_element_type=F32)


def kv_kernel(x_ref, w_ref, out_ref):
    out_ref[0] = nn(x_ref[...], w_ref[0]).astype(BF)


def project_kv(x, w_qkv):
    return pl.pallas_call(
        kv_kernel,
        grid=(2,),
        out_shape=shape((2, ROWS, WIDTH), BF),
        in_specs=[
            pl.BlockSpec((ROWS, D), lambda i: (0, 0)),
            pl.BlockSpec((1, D, WIDTH), lambda i: (i + 1, 0, 0)),
        ],
        out_specs=pl.BlockSpec((1, ROWS, WIDTH), lambda i: (i, 0, 0)),
        cost_estimate=pl.CostEstimate(
            flops=4 * ROWS * D * WIDTH, bytes_accessed=2 * 2**20, transcendentals=0
        ),
    )(x, w_qkv)


def attention_kernel(q_ref, u_ref, before_ref, own_ref, after_ref, bias_ref, acts_ref, gb_ref, go_ref, ga_ref):
    factor = HD**-0.5
    window = (before_ref, own_ref, after_ref)
    grads = (gb_ref, go_ref, ga_ref)
    lane = lax.broadcasted_iota(jnp.int32, (1, 128), 1)
    picks = [(lane < HD).astype(F32).astype(BF), (lane >= HD).astype(F32).astype(BF)]
    first = lax.broadcasted_iota(jnp.int32, (ROWS, 128), 1) < HD
    bias = [
        jnp.concatenate(
            [
                jnp.broadcast_to(bias_ref[b : b + 1, c * ROWS : (c + 1) * ROWS], (BLOCK, ROWS))
                for b in range(ROWS // BLOCK)
            ],
            axis=0,
        )
        for c in range(3)
    ]
    for pair in range(WIDTH // 128):
        cols = slice(pair * 128, (pair + 1) * 128)
        q2, u2 = q_ref[:, cols], u_ref[:, cols]
        keys = [w[0, :, cols] for w in window]
        values = [w[1, :, cols] for w in window]
        key_sum, value_sum = [None] * 3, [None] * 3
        att, dq = [], []
        for pick in picks:
            qm, um = q2 * pick, u2 * pick
            weights = [jnp.exp2(nt(qm, keys[c]) * (factor * LOG2E) + bias[c]) for c in range(3)]
            total = sum(jnp.sum(w, axis=1, keepdims=True) for w in weights)
            share = 1.0 / total
            probs = [w * share for w in weights]
            low = [p.astype(BF) for p in probs]
            dprob = [nt(um, values[c]) for c in range(3)]
            spread = sum(jnp.sum(p * d, axis=1, keepdims=True) for p, d in zip(probs, dprob))
            dscore = [(p * (d - spread) * factor).astype(BF) for p, d in zip(probs, dprob)]
            att.append(sum(nn(low[c], values[c]) for c in range(3)))
            dq.append(sum(nn(dscore[c], keys[c]) for c in range(3)))
            for c in range(3):
                dk, dv = tn(dscore[c], qm), tn(low[c], um)
                key_sum[c] = dk if key_sum[c] is None else key_sum[c] + dk
                value_sum[c] = dv if value_sum[c] is None else value_sum[c] + dv
        acts_ref[0, :, cols] = jnp.where(first, att[0], att[1]).astype(BF)
        acts_ref[1, :, cols] = jnp.where(first, dq[0], dq[1]).astype(BF)
        for c in range(3):
            grads[c][0, :, cols] = key_sum[c].astype(grads[c].dtype)
            grads[c][1, :, cols] = value_sum[c].astype(grads[c].dtype)


def out_kernel(idx_ref, acts_ref, w_ref, own_ref, *sent):
    head = idx_ref[3]
    for k in range(4):
        start = pl.multiple_of(lax.rem(head + k, 4) * WIDTH, WIDTH)
        part = nn(acts_ref[0], w_ref[:, pl.ds(start, WIDTH)])
        if k == 0:
            own_ref[...] = part
        else:
            sent[k - 1][...] = part.astype(BF)


def in_kernel(idx_ref, acts_ref, dkv_ref, w_ref, own_ref, *sent):
    head = idx_ref[3]
    for k in range(4):
        rows = pl.ds(pl.multiple_of(lax.rem(head + k, 4) * WIDTH, WIDTH), WIDTH)
        part = nt(acts_ref[1], w_ref[0, rows, :])
        part = part + nt(dkv_ref[0], w_ref[1, rows, :])
        part = part + nt(dkv_ref[1], w_ref[2, rows, :])
        if k == 0:
            own_ref[...] = part
        else:
            sent[k - 1][...] = part.astype(BF)


def weight_kernel(a_ref, a2_ref, b_ref, b2_ref, left_ref, right_ref, *outs, order):
    for k in range(4):
        rows = slice(k * 128, (k + 1) * 128)
        g = nn(a_ref[rows, :], left_ref[order[0]]) + nn(a2_ref[rows, :], right_ref[order[0]])
        outs[k][:, :WIDTH] = g.astype(outs[k].dtype)
        g = nn(b_ref[rows, :], left_ref[order[1]]) + nn(b2_ref[rows, :], right_ref[order[1]])
        outs[k][:, WIDTH:] = g.astype(outs[k].dtype)


def ysum_kernel(*refs):
    ins, outs = refs[:8], refs[8:]
    for part in range(2):
        cols = slice(part * 512, (part + 1) * 512)
        four = ins[part * 4 : part * 4 + 4]
        for o, (begin, end) in zip(outs, ((0, 16), (16, 48), (48, 80), (80, 112), (112, 128))):
            total = four[0][begin:end, :]
            for r in four[1:]:
                total = total + r[begin:end, :].astype(F32)
            o[:, cols] = total.astype(o.dtype)


def zsum_kernel(idx_ref, own_ref, r1_ref, r2_ref, r3_ref, r4_ref, out_ref):
    total = r1_ref[...].astype(F32) + r2_ref[...].astype(F32) + r3_ref[...].astype(F32)
    half = own_ref[...] + r4_ref[...].astype(F32)
    core = idx_ref[1]
    out_ref[0:16, :] = (total[0:16] + half * (1 - core).astype(F32)).astype(BF)
    out_ref[16:32, :] = (total[16:32] + half * core.astype(F32)).astype(BF)


def place_kernel(idx_ref, *refs):
    mine, other, qkv_ref, out_ref, turned = refs[:4], refs[4:8], refs[8], refs[9], refs[10]
    z, core, y = idx_ref[0], idx_ref[1], idx_ref[2]
    for side, blocks in ((core, mine), (1 - core, other)):
        step = 2 * side - 1
        for k in range(4):
            base = lax.rem(y + 4 - k, 4) * 256
            pieces = [(0, 16, z * 32 + side * 16)]
            for j in (1, 2, 3):
                pieces.append((32 * j - 16, 32, lax.rem(z + step * j + 8, 8) * 32))
            pieces.append((112, 16, lax.rem(z + 4, 8) * 32 + side * 16))
            for begin, count, place in pieces:
                rows = pl.ds(pl.multiple_of(base + place, 16), count)
                piece = blocks[k][begin : begin + count, :].astype(F32)
                qkv_ref[0, rows, :] = piece[:, 0:256]
                turned[rows, :] = piece[:, 256:512]
                qkv_ref[1, rows, :] = piece[:, 512:768]
                qkv_ref[2, rows, :] = piece[:, 768:1024]
    out_ref[...] = turned[...].T


def row_of(z, y, side):
    p = jnp.arange(128, dtype=jnp.int32)
    j = (p - 16) // 32 + 1
    middle = (z + (1 - 2 * side) * j) % 8 * 32 + (p - 16) % 32
    row = jnp.where(
        p < 16,
        z * 32 + side * 16 + p,
        jnp.where(p < 112, middle, (z + 4) % 8 * 32 + side * 16 + p - 112),
    )
    k = jnp.arange(4, dtype=jnp.int32)
    return (((y + k) % 4 * 256)[:, None] + row[None, :]).reshape(512)


def per_device(tokens, neighbours, counts, w_qkv, w_out, cotangent):
    x, listed, occupied, cot = tokens[0], neighbours[0], counts[0], cotangent[0]
    spatial, head, y = (lax.axis_index(a) for a in ("spatial", "head", "dp"))
    z, core = spatial // 2, spatial % 2
    idx = jnp.stack([z, core, y, head]).astype(jnp.int32)
    n = 16
    up = [(i, i + 1) for i in range(n - 1)]
    down = [(i + 1, i) for i in range(n - 1)]
    swap = [(i, i ^ 1) for i in range(n)]

    def spread_z(j):
        return [(i, (i // 2 + (j if i % 2 == 0 else -j)) % 8 * 2 + i % 2) for i in range(n)]

    def ring(k):
        return [(i, (i + k) % 4) for i in range(4)]

    def swapped(a):
        return lax.ppermute(a, "spatial", swap)

    kv = project_kv(x, w_qkv)
    before = lax.ppermute(kv, "spatial", up)
    after = lax.ppermute(kv, "spatial", down)

    q = jnp.dot(x, w_qkv[0], preferred_element_type=F32).astype(BF)
    u = lax.dot_general(cot, w_out, (((1,), (1,)), ((), ())), preferred_element_type=F32).astype(BF)

    blocks = ROWS // BLOCK
    near = 3 * blocks
    ids = spatial * blocks - REACH + jnp.arange(near, dtype=jnp.int32)
    hit = jnp.any(listed[:, :, None] == ids[None, None, :], axis=1) & (ids >= 0)[None, :]
    padded = jnp.pad(occupied, (REACH, REACH))
    limit = lax.dynamic_slice_in_dim(padded, spatial * blocks, near, 0)
    limit = jnp.where(hit, limit[None, :], 0)
    slots = jnp.arange(BLOCK, dtype=jnp.int32)
    bias = jnp.where(slots[None, None, :] < limit[:, :, None], 0.0, -1e30).astype(F32)
    bias = bias.reshape(blocks, near * BLOCK)

    features = jnp.arange(D, dtype=jnp.int32)[:, None]
    pick_mine = (features == row_of(z, y, core)[None, :]).astype(BF)
    pick_other = (features == row_of(z, y, 1 - core)[None, :]).astype(BF)

    def picked(pick, a):
        return lax.dot_general(pick, a, (((0,), (1,)), ((), ())), preferred_element_type=F32).astype(BF)

    x_mine, x_other = picked(pick_mine, x), swapped(picked(pick_other, x))
    c_mine, c_other = picked(pick_mine, cot), swapped(picked(pick_other, cot))

    acts, grad_b, grad_o, grad_a = call(
        attention_kernel,
        [
            shape((2, ROWS, WIDTH), BF),
            shape((2, ROWS, WIDTH), BF),
            shape((2, ROWS, WIDTH), F32),
            shape((2, ROWS, WIDTH), BF),
        ],
        [q, u, before, kv, after, bias],
        10 * 256 * 768 * 256,
        vmem=32,
    )
    from_after = lax.ppermute(grad_b, "spatial", down)
    from_before = lax.ppermute(grad_a, "spatial", up)
    acts_other = swapped(acts)

    def sent_shapes():
        return [shape((ROWS, WIDTH), F32)] + [shape((ROWS, WIDTH), BF)] * 3

    def head_sum(parts, base):
        total = parts[0]
        for k in (1, 2, 3):
            total = total + lax.ppermute(parts[k], "head", ring(k)).astype(F32)
        own = lax.dynamic_slice_in_dim(base, head * WIDTH, WIDTH, 1)
        return (own.astype(F32) + total).astype(BF)

    with_idx = [SMEM] + [VMEM] * 2
    out_parts = call(out_kernel, sent_shapes(), [idx, acts, w_out], 2 * ROWS * WIDTH * D, with_idx)
    layer_out = head_sum(out_parts, x)

    part_shapes = [shape((128, 512), F32)] + [shape((128, 512), BF)] * 3

    def to_y(parts):
        return [parts[0]] + [lax.ppermute(parts[k], "dp", ring(k)) for k in (1, 2, 3)]

    g1 = to_y(
        call(
            functools.partial(weight_kernel, order=(1, 0)),
            part_shapes,
            [x_mine, x_other, c_mine, c_other, acts, acts_other],
            4 * 512 * 512 * 256,
        )
    )

    dkv = (grad_o + from_after.astype(F32) + from_before.astype(F32)).astype(BF)
    dkv_other = swapped(dkv)
    in_parts = call(
        in_kernel, sent_shapes(), [idx, acts, dkv, w_qkv], 6 * ROWS * WIDTH * D, [SMEM] + [VMEM] * 3
    )
    g2 = to_y(
        call(
            functools.partial(weight_kernel, order=(0, 1)),
            part_shapes,
            [x_mine, x_other, x_mine, x_other, dkv, dkv_other],
            4 * 512 * 512 * 256,
        )
    )
    grad_tokens = head_sum(in_parts, cot)

    own, *to_z = call(
        ysum_kernel,
        [shape((16, D), F32)] + [shape((32, D), BF)] * 3 + [shape((16, D), BF)],
        g1 + g2,
        2**20,
    )
    arrived = [lax.ppermute(a, "spatial", spread_z(j)) for j, a in zip((1, 2, 3, 4), to_z)]
    chunk = call(
        zsum_kernel, [shape((32, D), BF)], [idx, own] + arrived, 2**18, [SMEM] + [VMEM] * 5
    )[0]
    chunk = (chunk.astype(F32) + swapped(chunk).astype(F32)).astype(BF)
    half = lax.dynamic_slice_in_dim(chunk, core * 16, 16, 0)
    pieces = [half] + [lax.ppermute(chunk, "spatial", spread_z(j)) for j in (1, 2, 3)]
    pieces.append(lax.ppermute(half, "spatial", spread_z(4)))
    column = jnp.concatenate(pieces, axis=0)
    mine = [column] + [lax.ppermute(column, "dp", ring(k)) for k in (1, 2, 3)]
    other = [swapped(a) for a in mine]
    grad_qkv, grad_out = call(
        place_kernel,
        [shape((3, D, WIDTH), F32), shape((WIDTH, D), F32)],
        [idx] + mine + other,
        2**20,
        [SMEM] + [VMEM] * 8,
        scratch=[pltpu.VMEM((D, WIDTH), F32)],
    )
    return layer_out[None], grad_tokens[None], grad_qkv, grad_out


def solution(mesh):
    in_specs = (
        P("dp", "spatial", None),
        P("dp", "spatial", None),
        P("dp", None),
        P(None, None, "head"),
        P("head", None),
        P("dp", "spatial", None),
    )
    out_specs = (
        P("dp", "spatial", "head"),
        P("dp", "spatial", "head"),
        P(None, None, "head"),
        P("head", None),
    )
    return jax.shard_map(
        per_device, mesh=mesh, in_specs=in_specs, out_specs=out_specs, check_vma=False
    )
```

```python
import jax
import jax.numpy as jnp
from jax import lax
from jax.experimental import pallas as pl
from jax.experimental.pallas import tpu as pltpu
from jax.sharding import PartitionSpec as P

HD = 64
BLOCK = 64
ROWS = 256
WIDTH = 256
D = 1024
PLACE_ORDER = (0, 3, 1, 2)
LOG2E = 1.4426950408889634
BF = jnp.bfloat16
F32 = jnp.float32
VMEM = pl.BlockSpec(memory_space=pltpu.VMEM)
ANY = pl.BlockSpec(memory_space=pl.ANY)
HBM = pl.BlockSpec(memory_space=pltpu.HBM)


def call(kernel, outs, operands, flops, in_specs=None, scratch=(), vmem=24, after=(), out_specs=None):
    moved = sum(a.size * a.dtype.itemsize for a in operands)
    moved += sum(o.size * o.dtype.itemsize for o in outs)
    count = len(operands)

    def body(*refs):
        kernel(*refs[:count], *refs[count + len(after) :])

    return pl.pallas_call(
        body,
        out_shape=outs,
        in_specs=(in_specs or [VMEM] * count) + [ANY] * len(after),
        out_specs=out_specs or [VMEM] * len(outs),
        scratch_shapes=list(scratch),
        compiler_params=pltpu.CompilerParams(vmem_limit_bytes=vmem * 2**20),
        cost_estimate=pl.CostEstimate(flops=flops, bytes_accessed=moved, transcendentals=0),
    )(*operands, *after)


def shape(dims, kind):
    return jax.ShapeDtypeStruct(dims, kind)


def nn(a, b):
    return lax.dot_general(a, b, (((1,), (0,)), ((), ())), preferred_element_type=F32)


def nt(a, b):
    return lax.dot_general(a, b, (((1,), (1,)), ((), ())), preferred_element_type=F32)


def tn(a, b):
    return lax.dot_general(a, b, (((0,), (0,)), ((), ())), preferred_element_type=F32)


def place_of():
    spatial = lax.axis_index("spatial")
    return spatial >> 1, spatial & 1, lax.axis_index("dp"), lax.axis_index("head")


def picker(side):
    z, _, y, _ = place_of()
    c = lax.broadcasted_iota(jnp.int32, (512, 1), 0)
    k, m = c >> 7, (c >> 4) & 7
    chunk = z ^ (2 * (m & 3) + (m >> 2))
    row = (y ^ k) * 256 + side * 128 + chunk * 16 + (c & 15)
    feature = lax.broadcasted_iota(jnp.int32, (512, D), 1)
    return (feature == row).astype(F32).astype(BF)


def pick_rows(side, x_ref, cot_ref, out_ref):
    pick = picker(side)
    out_ref[0] = nt(pick, x_ref[...]).astype(BF)
    out_ref[1] = nt(pick, cot_ref[...]).astype(BF)


def first_kernel(*refs):
    inputs, (kv_ref, q_ref, u_ref, xc_ref), held, sems = refs[:4], refs[4:8], refs[8:12], refs[12]
    x_ref, wqkv_ref, wo_ref, cot_ref = held
    loads = [
        (inputs[0], x_ref),
        (inputs[1].at[1], wqkv_ref.at[1]),
        (inputs[1].at[2], wqkv_ref.at[2]),
        (inputs[1].at[0], wqkv_ref.at[0]),
        (inputs[2], wo_ref),
        (inputs[3], cot_ref),
    ]
    loads = [pltpu.make_async_copy(a, b, sems.at[i]) for i, (a, b) in enumerate(loads)]
    for load in loads:
        load.start()
    for load in loads[:3]:
        load.wait()
    kv_ref[0] = nn(x_ref[...], wqkv_ref[1]).astype(BF)
    kv_ref[1] = nn(x_ref[...], wqkv_ref[2]).astype(BF)
    for load in loads[3:]:
        load.wait()
    q_ref[...] = nn(x_ref[...], wqkv_ref[0]).astype(BF)
    u_ref[...] = nt(cot_ref[...], wo_ref[...]).astype(BF)

    pick_rows(1 - place_of()[1], x_ref, cot_ref, xc_ref)


def mine_kernel(x_ref, cot_ref, xc_ref):
    pick_rows(place_of()[1], x_ref, cot_ref, xc_ref)


def attention_kernel(q_ref, u_ref, far_ref, own_ref, mate_ref, bias_ref, acts_ref, gf_ref, go_ref, gm_ref):
    factor = HD**-0.5
    window = (far_ref, own_ref, mate_ref)
    grads = (gf_ref, go_ref, gm_ref)
    lane = lax.broadcasted_iota(jnp.int32, (1, 128), 1)
    picks = [(lane < HD).astype(F32).astype(BF), (lane >= HD).astype(F32).astype(BF)]
    first = lax.broadcasted_iota(jnp.int32, (ROWS, 128), 1) < HD
    bias = [
        jnp.concatenate(
            [
                jnp.broadcast_to(bias_ref[b : b + 1, c * ROWS : (c + 1) * ROWS], (BLOCK, ROWS))
                for b in range(ROWS // BLOCK)
            ],
            axis=0,
        )
        for c in range(3)
    ]
    for pair in range(WIDTH // 128):
        cols = slice(pair * 128, (pair + 1) * 128)
        q2, u2 = q_ref[:, cols], u_ref[:, cols]
        keys = [w[0, :, cols] for w in window]
        values = [w[1, :, cols] for w in window]
        key_sum, value_sum = [None] * 3, [None] * 3
        att, dq = [], []
        for pick in picks:
            qm, um = q2 * pick, u2 * pick
            weights = [jnp.exp2(nt(qm, keys[c]) * (factor * LOG2E) + bias[c]) for c in range(3)]
            total = sum(jnp.sum(w, axis=1, keepdims=True) for w in weights)
            share = 1.0 / total
            probs = [w * share for w in weights]
            low = [p.astype(BF) for p in probs]
            dprob = [nt(um, values[c]) for c in range(3)]
            spread = sum(jnp.sum(p * d, axis=1, keepdims=True) for p, d in zip(probs, dprob))
            dscore = [(p * (d - spread) * factor).astype(BF) for p, d in zip(probs, dprob)]
            att.append(sum(nn(low[c], values[c]) for c in range(3)))
            dq.append(sum(nn(dscore[c], keys[c]) for c in range(3)))
            for c in range(3):
                dk, dv = tn(dscore[c], qm), tn(low[c], um)
                key_sum[c] = dk if key_sum[c] is None else key_sum[c] + dk
                value_sum[c] = dv if value_sum[c] is None else value_sum[c] + dv
        acts_ref[0, :, cols] = jnp.where(first, att[0], att[1]).astype(BF)
        acts_ref[1, :, cols] = jnp.where(first, dq[0], dq[1]).astype(BF)
        for c in range(3):
            grads[c][0, :, cols] = key_sum[c].astype(grads[c].dtype)
            grads[c][1, :, cols] = value_sum[c].astype(grads[c].dtype)


def head_kernel(acts_ref, dkv_ref, wo_ref, w_ref, own_ref, *sent):
    head = place_of()[3]
    for k in range(4):
        span = pl.ds(pl.multiple_of((head ^ k) * WIDTH, WIDTH), WIDTH)
        out = nn(acts_ref[0], wo_ref[:, span])
        grad = nt(acts_ref[1], w_ref[0, span, :])
        grad = grad + nt(dkv_ref[0], w_ref[1, span, :])
        grad = grad + nt(dkv_ref[1], w_ref[2, span, :])
        to = own_ref if k == 0 else sent[k - 1]
        to[0] = out.astype(to.dtype)
        to[1] = grad.astype(to.dtype)


def head_sum_kernel(own_ref, r1_ref, r2_ref, r3_ref, x_ref, cot_ref, out_ref, grad_ref, token_ref):
    token_ref[...] = jnp.zeros_like(token_ref)
    span = pl.ds(pl.multiple_of(place_of()[3] * WIDTH, WIDTH), WIDTH)
    for i, (base, to) in enumerate(((x_ref, out_ref), (cot_ref, grad_ref))):
        total = own_ref[i] + r1_ref[i].astype(F32) + r2_ref[i].astype(F32) + r3_ref[i].astype(F32)
        to[...] = (base[:, span].astype(F32) + total).astype(BF)


def dkv_kernel(own_ref, a_ref, b_ref, out_ref):
    out_ref[...] = (own_ref[...] + a_ref[...].astype(F32) + b_ref[...].astype(F32)).astype(BF)


def early_kernel(mine_ref, other_ref, left_ref, right_ref, own_ref, rest_ref):
    for i, (side, act) in enumerate(((0, 1), (1, 0))):
        cols = slice(i * WIDTH, (i + 1) * WIDTH)
        g = nn(mine_ref[side], left_ref[act]) + nn(other_ref[side], right_ref[act])
        own_ref[:, cols] = g[:128]
        rest_ref[:, cols] = g[128:].astype(BF)


def late_kernel(mine_ref, other_ref, left_ref, right_ref, own1_ref, rest1_ref, own_ref, *sent):
    own_ref[:, : 2 * WIDTH] = own1_ref[...]
    for k in range(3):
        sent[k][:, : 2 * WIDTH] = rest1_ref[k * 128 : (k + 1) * 128, :]
    for i in range(2):
        cols = slice((2 + i) * WIDTH, (3 + i) * WIDTH)
        g = nn(mine_ref[0], left_ref[i]) + nn(other_ref[0], right_ref[i])
        own_ref[:, cols] = g[:128]
        for k in range(3):
            sent[k][:, cols] = g[(k + 1) * 128 : (k + 2) * 128].astype(BF)


def ysum_kernel(own_ref, r1_ref, r2_ref, r3_ref, kept_ref, sent_ref):
    total = own_ref[...] + r1_ref[...].astype(F32) + r2_ref[...].astype(F32) + r3_ref[...].astype(F32)
    kept_ref[...] = total[:64]
    sent_ref[...] = total[64:].astype(BF)


def pair_sum_kernel(kept_ref, r_ref, own_ref, *sent):
    total = kept_ref[...] + r_ref[...].astype(F32)
    own_ref[...] = total[:16]
    for i in range(3):
        sent[i][...] = total[16 * i + 16 : 16 * i + 32].astype(BF)


def chunk_kernel(own_ref, r1_ref, r2_ref, r3_ref, out_ref):
    total = own_ref[...] + r1_ref[...].astype(F32) + r2_ref[...].astype(F32) + r3_ref[...].astype(F32)
    out_ref[...] = total.astype(BF)


def join_kernel(*refs):
    begin = 0
    for r in refs[:-1]:
        refs[-1][begin : begin + r.shape[0], :] = r[...]
        begin += r.shape[0]


def place_kernel(*refs):
    mine, other, (qkv_ref, out_ref, held, turned, sems) = refs[:4], refs[4:8], refs[8:]
    z, core, y, _ = place_of()
    copies = []
    for k in PLACE_ORDER:
        block = pl.ds(pl.multiple_of((y ^ k) * 256, 256), 256)
        for array, column in ((3, 1), (0, 0), (1, 2), (2, 3)):
            cols = slice(column * WIDTH, (column + 1) * WIDTH)
            for side, blocks in ((core, mine), (1 - core, other)):
                for m in range(8):
                    chunk = z ^ (2 * (m & 3) + (m >> 2))
                    rows = pl.ds(pl.multiple_of(side * 128 + chunk * 16, 16), 16)
                    held[k, array, rows, :] = blocks[k][m * 16 : m * 16 + 16, cols].astype(F32)
            if array == 3:
                turned[k] = held[k, 3].T
                copy = pltpu.make_async_copy(turned.at[k], out_ref.at[:, block], sems.at[k, 3])
            else:
                copy = pltpu.make_async_copy(
                    held.at[k, array], qkv_ref.at[array, block], sems.at[k, array]
                )
            copy.start()
            copies.append(copy)
    for copy in copies:
        copy.wait()


def per_device(tokens, neighbours, counts, w_qkv, w_out, cotangent):
    x, listed, occupied, cot = tokens[0], neighbours[0], counts[0], cotangent[0]
    n = 16
    swap = [(i, i ^ 1) for i in range(n)]
    cross = [(i, i if i in (0, n - 1) else i + 1 if i % 2 else i - 1) for i in range(n)]

    def pair_z(k):
        return [(i, i ^ (2 * k)) for i in range(n)]

    def pair(k):
        return [(i, i ^ k) for i in range(4)]

    def swapped(a):
        return lax.ppermute(a, "spatial", swap)

    kv, q, u, xc_sent = call(
        first_kernel,
        [
            shape((2, ROWS, WIDTH), BF),
            shape((ROWS, WIDTH), BF),
            shape((ROWS, WIDTH), BF),
            shape((2, 512, ROWS), BF),
        ],
        [x, w_qkv, w_out, cot],
        12 * ROWS * D * WIDTH,
        [HBM] * 4,
        scratch=[
            pltpu.VMEM((ROWS, D), BF),
            pltpu.VMEM((3, D, WIDTH), BF),
            pltpu.VMEM((WIDTH, D), BF),
            pltpu.VMEM((ROWS, D), BF),
            pltpu.SemaphoreType.DMA((6,)),
        ],
        vmem=53,
    )
    far_kv = lax.ppermute(kv, "spatial", cross)
    mate_kv = swapped(kv)

    xc_other = swapped(xc_sent)

    spatial = lax.axis_index("spatial")
    base, side = spatial * 4, 1 - 2 * (spatial % 2)
    ids = (base + jnp.array([-4, 0, 4]) * side)[:, None] + jnp.arange(4)
    ids = ids.reshape(12).astype(jnp.int32)
    hit = jnp.any(listed[:, :, None] == ids[None, None, :], axis=1)
    table = jnp.arange(occupied.shape[0], dtype=jnp.int32)
    limit = jnp.sum(jnp.where(ids[:, None] == table[None, :], occupied[None, :], 0), axis=1)
    limit = jnp.where(hit, limit[None, :], 0)
    slots = jnp.arange(BLOCK, dtype=jnp.int32)
    bias = jnp.where(slots[None, None, :] < limit[:, :, None], 0.0, -1e30).astype(F32)
    bias = bias.reshape(4, 12 * BLOCK)

    acts, grad_far, grad_own, grad_mate = call(
        attention_kernel,
        [
            shape((2, ROWS, WIDTH), BF),
            shape((2, ROWS, WIDTH), BF),
            shape((2, ROWS, WIDTH), F32),
            shape((2, ROWS, WIDTH), BF),
        ],
        [q, u, far_kv, kv, mate_kv, bias],
        10 * 256 * 768 * 256,
        vmem=32,
    )
    from_far = lax.ppermute(grad_far, "spatial", cross)
    from_mate = swapped(grad_mate)
    acts_other = swapped(acts)
    xc_mine = call(
        mine_kernel,
        [shape((2, 512, ROWS), BF)],
        [x, cot],
        4 * 512 * 256 * D,
        after=[acts],
    )[0]
    early = call(
        early_kernel,
        [shape((128, 512), F32), shape((384, 512), BF)],
        [xc_mine, xc_other, acts, acts_other],
        4 * 512 * 512 * 256,
    )
    dkv = call(
        dkv_kernel,
        [shape((2, ROWS, WIDTH), BF)],
        [grad_own, from_far, from_mate],
        2**18,
        after=[early[0]],
    )[0]
    own, *to_y = call(
        late_kernel,
        [shape((128, D), F32)] + [shape((128, D), BF)] * 3,
        [xc_mine, xc_other, dkv, swapped(dkv), *early],
        4 * 512 * 512 * 256,
    )
    from_y = [lax.ppermute(a, "dp", pair(k)) for k, a in zip((1, 2, 3), to_y)]

    head_own, *to_head = call(
        head_kernel,
        [shape((2, ROWS, WIDTH), F32)] + [shape((2, ROWS, WIDTH), BF)] * 3,
        [acts, dkv, w_out, w_qkv],
        8 * ROWS * WIDTH * D,
        after=[own],
    )
    from_head = [lax.ppermute(a, "head", pair(k)) for k, a in zip((1, 2, 3), to_head)]

    kept, sent = call(
        ysum_kernel,
        [shape((64, D), F32), shape((64, D), BF)],
        [own] + from_y,
        2**20,
        after=[from_head[0], from_head[2]],
    )
    own, *to_z = call(
        pair_sum_kernel,
        [shape((16, D), F32)] + [shape((16, D), BF)] * 3,
        [kept, lax.ppermute(sent, "spatial", pair_z(1))],
        2**18,
    )
    from_z = [lax.ppermute(a, "spatial", pair_z(k)) for k, a in zip((2, 4, 6), to_z)]
    chunk = call(chunk_kernel, [shape((16, D), BF)], [own] + from_z, 2**16)[0]
    pieces = [chunk] + [lax.ppermute(chunk, "spatial", pair_z(k)) for k in (2, 4, 6)]
    layer_out, grad_tokens, token = call(
        head_sum_kernel,
        [shape((ROWS, WIDTH), BF)] * 2 + [shape((8, 128), F32)],
        [head_own, *from_head, x, cot],
        2**20,
        after=[chunk],
    )
    half = call(join_kernel, [shape((64, D), BF)], pieces, 2**16)[0]
    column = call(
        join_kernel,
        [shape((128, D), BF)],
        [half, lax.ppermute(half, "spatial", pair_z(1))],
        2**16,
        after=[token],
    )[0]
    mine = [column] + [lax.ppermute(column, "dp", pair(k)) for k in (1, 2, 3)]
    other = [swapped(a) for a in mine]
    grad_qkv, grad_out = call(
        place_kernel,
        [shape((3, D, WIDTH), F32), shape((WIDTH, D), F32)],
        mine + other,
        2**20,
        scratch=[
            pltpu.VMEM((4, 4, 256, WIDTH), F32),
            pltpu.VMEM((4, WIDTH, 256), F32),
            pltpu.SemaphoreType.DMA((4, 4)),
        ],
        out_specs=[ANY, ANY],
    )
    return layer_out[None], grad_tokens[None], grad_qkv, grad_out


def solution(mesh):
    in_specs = (
        P("dp", "spatial", None),
        P("dp", "spatial", None),
        P("dp", None),
        P(None, None, "head"),
        P("head", None),
        P("dp", "spatial", None),
    )
    out_specs = (
        P("dp", "spatial", "head"),
        P("dp", "spatial", "head"),
        P(None, None, "head"),
        P("head", None),
    )
    return jax.shard_map(
        per_device, mesh=mesh, in_specs=in_specs, out_specs=out_specs, check_vma=False
    )
```

```python
import functools

import jax
import jax.numpy as jnp
from jax import lax
from jax.experimental import pallas as pl
from jax.experimental.pallas import tpu as pltpu
from jax.sharding import PartitionSpec as P

HD = 64
BLOCK = 64
ROWS = 256
WIDTH = 256
D = 1024
PLACE_ORDER = (0, 2, 3, 1)
LOG2E = 1.4426950408889634
BF = jnp.bfloat16
F32 = jnp.float32
VMEM = pl.BlockSpec(memory_space=pltpu.VMEM)
ANY = pl.BlockSpec(memory_space=pl.ANY)
HBM = pl.BlockSpec(memory_space=pltpu.HBM)


def call(kernel, outs, operands, flops, in_specs=None, scratch=(), vmem=24, after=(), out_specs=None):
    moved = sum(a.size * a.dtype.itemsize for a in operands)
    moved += sum(o.size * o.dtype.itemsize for o in outs)
    count = len(operands)

    def body(*refs):
        kernel(*refs[:count], *refs[count + len(after) :])

    return pl.pallas_call(
        body,
        out_shape=outs,
        in_specs=(in_specs or [VMEM] * count) + [ANY] * len(after),
        out_specs=out_specs or [VMEM] * len(outs),
        scratch_shapes=list(scratch),
        compiler_params=pltpu.CompilerParams(vmem_limit_bytes=int(vmem * 2**20)),
        cost_estimate=pl.CostEstimate(flops=flops, bytes_accessed=moved, transcendentals=0),
    )(*operands, *after)


def shape(dims, kind):
    return jax.ShapeDtypeStruct(dims, kind)


def nn(a, b):
    return lax.dot_general(a, b, (((1,), (0,)), ((), ())), preferred_element_type=F32)


def nt(a, b):
    return lax.dot_general(a, b, (((1,), (1,)), ((), ())), preferred_element_type=F32)


def tn(a, b):
    return lax.dot_general(a, b, (((0,), (0,)), ((), ())), preferred_element_type=F32)


def place_of():
    spatial = lax.axis_index("spatial")
    return spatial >> 1, spatial & 1, lax.axis_index("dp"), lax.axis_index("head")


def picker(side):
    z, _, y, _ = place_of()
    c = lax.broadcasted_iota(jnp.int32, (512, 1), 0)
    k, m = c >> 7, (c >> 5) & 3
    row = (y ^ k) * 256 + side * 128 + ((z & 3) ^ m) * 32 + (c & 31)
    feature = lax.broadcasted_iota(jnp.int32, (512, D), 1)
    return (feature == row).astype(F32).astype(BF)


def pick_rows(side, x_ref, cot_ref, out_ref):
    pick = picker(side)
    out_ref[0] = nt(pick, x_ref[...]).astype(BF)
    out_ref[1] = nt(pick, cot_ref[...]).astype(BF)


def fetch(pairs, sems):
    loads = [pltpu.make_async_copy(a, b, sems.at[i]) for i, (a, b) in enumerate(pairs)]
    for load in loads:
        load.start()
    return loads


def kv_kernel(x_hbm, w_hbm, out_ref, x_ref, w_ref, sems):
    pairs = [(x_hbm, x_ref), (w_hbm.at[1], w_ref.at[0]), (w_hbm.at[2], w_ref.at[1])]
    x_load, *loads = fetch(pairs, sems)
    x_load.wait()
    for i in range(2):
        loads[i].wait()
        out_ref[i] = nn(x_ref[...], w_ref[i]).astype(BF)


def prep_kernel(
    x_hbm, w_hbm, wo_hbm, cot_hbm, blocks_ref,
    q_ref, u_ref, xc_ref, bias_ref, x_ref, w_ref, wo_ref, cot_ref, sems
):
    pairs = [(x_hbm, x_ref), (w_hbm.at[0], w_ref), (cot_hbm, cot_ref), (wo_hbm, wo_ref)]
    x_load, w_load, cot_load, wo_load = fetch(pairs, sems)

    z, core, _, _ = place_of()
    base = (z * 2 + core) * 4
    starts = (base - 4 + 8 * core, base, base + 4 - 8 * core)
    lane = lax.broadcasted_iota(jnp.int32, (4, 128), 1)
    slot = (lane & (BLOCK - 1)).astype(F32)
    table = lax.broadcasted_iota(jnp.int32, (1, 128), 1)
    listed, occupied = blocks_ref[0:4, :], blocks_ref[4:5, :].astype(F32)

    def limit(block):
        hit = jnp.max(jnp.where(listed == block, 1.0, 0.0), axis=1, keepdims=True)
        return hit * jnp.sum(jnp.where(table == block, occupied, 0.0), axis=1, keepdims=True)

    for w in range(0, 12, 2):
        block = starts[w // 4] + w % 4
        edge = jnp.where(lane < BLOCK, limit(block), limit(block + 1))
        bias_ref[:, w * BLOCK : (w + 2) * BLOCK] = jnp.where(slot < edge, 0.0, -1e30)

    x_load.wait()
    w_load.wait()
    q_ref[...] = nn(x_ref[...], w_ref[...]).astype(BF)
    cot_load.wait()
    wo_load.wait()
    u_ref[...] = nt(cot_ref[...], wo_ref[...]).astype(BF)
    pick_rows(1 - core, x_ref, cot_ref, xc_ref)


def mine_kernel(x_ref, cot_ref, xc_ref):
    pick_rows(place_of()[1], x_ref, cot_ref, xc_ref)


def attention_kernel(q_ref, u_ref, mate_ref, own_ref, far_ref, bias_ref, acts_ref, gf_ref, go_ref, gm_ref):
    factor = HD**-0.5
    window = (far_ref, own_ref, mate_ref)
    grads = (gf_ref, go_ref, gm_ref)
    lane = lax.broadcasted_iota(jnp.int32, (1, 128), 1)
    picks = [(lane < HD).astype(F32).astype(BF), (lane >= HD).astype(F32).astype(BF)]
    first = lax.broadcasted_iota(jnp.int32, (ROWS, 128), 1) < HD
    bias = [
        jnp.concatenate(
            [
                jnp.broadcast_to(bias_ref[b : b + 1, c * ROWS : (c + 1) * ROWS], (BLOCK, ROWS))
                for b in range(ROWS // BLOCK)
            ],
            axis=0,
        )
        for c in range(3)
    ]
    for pair in range(WIDTH // 128):
        cols = slice(pair * 128, (pair + 1) * 128)
        q2, u2 = q_ref[:, cols], u_ref[:, cols]
        keys = [w[0, :, cols] for w in window]
        values = [w[1, :, cols] for w in window]
        key_sum, value_sum = [None] * 3, [None] * 3
        att, dq = [], []
        for pick in picks:
            qm, um = q2 * pick, u2 * pick
            weights = [jnp.exp2(nt(qm, keys[c]) * (factor * LOG2E) + bias[c]) for c in range(3)]
            total = sum(jnp.sum(w, axis=1, keepdims=True) for w in weights)
            share = 1.0 / total
            probs = [w * share for w in weights]
            low = [p.astype(BF) for p in probs]
            dprob = [nt(um, values[c]) for c in range(3)]
            spread = sum(jnp.sum(p * d, axis=1, keepdims=True) for p, d in zip(probs, dprob))
            dscore = [(p * (d - spread) * factor).astype(BF) for p, d in zip(probs, dprob)]
            att.append(sum(nn(low[c], values[c]) for c in range(3)))
            dq.append(sum(nn(dscore[c], keys[c]) for c in range(3)))
            for c in range(3):
                dk, dv = tn(dscore[c], qm), tn(low[c], um)
                key_sum[c] = dk if key_sum[c] is None else key_sum[c] + dk
                value_sum[c] = dv if value_sum[c] is None else value_sum[c] + dv
        acts_ref[0, :, cols] = jnp.where(first, att[0], att[1]).astype(BF)
        acts_ref[1, :, cols] = jnp.where(first, dq[0], dq[1]).astype(BF)
        for c in range(3):
            grads[c][0, :, cols] = key_sum[c].astype(grads[c].dtype)
            grads[c][1, :, cols] = value_sum[c].astype(grads[c].dtype)


def head_kernel(acts_ref, dkv_ref, wo_ref, w_ref, *outs, parts):
    head = place_of()[3]
    for to, k in zip(outs, parts):
        span = pl.ds(pl.multiple_of((head ^ k) * WIDTH, WIDTH), WIDTH)
        out = nn(acts_ref[0], wo_ref[:, span])
        grad = nt(acts_ref[1], w_ref[0, span, :])
        grad = grad + nt(dkv_ref[0], w_ref[1, span, :])
        grad = grad + nt(dkv_ref[1], w_ref[2, span, :])
        to[0] = out.astype(to.dtype)
        to[1] = grad.astype(to.dtype)


def head_sum_kernel(own_ref, r1_ref, r2_ref, r3_ref, x_ref, cot_ref, out_ref, grad_ref, token_ref):
    token_ref[...] = jnp.zeros_like(token_ref)
    span = pl.ds(pl.multiple_of(place_of()[3] * WIDTH, WIDTH), WIDTH)
    for i, (base, to) in enumerate(((x_ref, out_ref), (cot_ref, grad_ref))):
        total = own_ref[i] + r1_ref[i].astype(F32) + r2_ref[i].astype(F32) + r3_ref[i].astype(F32)
        to[...] = (base[:, span].astype(F32) + total).astype(BF)


def dkv_kernel(own_ref, a_ref, b_ref, out_ref):
    out_ref[...] = (own_ref[...] + a_ref[...].astype(F32) + b_ref[...].astype(F32)).astype(BF)


def dkv_kernel(own_ref, a_ref, b_ref, out_ref):
    out_ref[...] = (own_ref[...] + a_ref[...].astype(F32) + b_ref[...].astype(F32)).astype(BF)


def weight_kernel(mine_ref, other_ref, left_ref, right_ref, own_ref, *sent, terms):
    for i, (side, act) in enumerate(terms):
        cols = slice(i * WIDTH, (i + 1) * WIDTH)
        g = nn(mine_ref[side], left_ref[act]) + nn(other_ref[side], right_ref[act])
        own_ref[:, cols] = g[:128]
        for k in range(3):
            sent[k][:, cols] = g[(k + 1) * 128 : (k + 2) * 128].astype(BF)


def dkv_kernel(own_ref, a_ref, b_ref, out_ref):
    out_ref[...] = (own_ref[...] + a_ref[...].astype(F32) + b_ref[...].astype(F32)).astype(BF)


def early_kernel(mine_ref, other_ref, left_ref, right_ref, own_ref, rest_ref):
    for i, (side, act) in enumerate(((0, 1), (1, 0))):
        cols = slice(i * WIDTH, (i + 1) * WIDTH)
        g = nn(mine_ref[side], left_ref[act]) + nn(other_ref[side], right_ref[act])
        own_ref[:, cols] = g[:128]
        rest_ref[:, cols] = g[128:].astype(BF)


def late_kernel(mine_ref, other_ref, left_ref, right_ref, own1_ref, rest1_ref, own_ref, *sent):
    own_ref[:, : 2 * WIDTH] = own1_ref[...]
    for k in range(3):
        sent[k][:, : 2 * WIDTH] = rest1_ref[k * 128 : (k + 1) * 128, :]
    for i in range(2):
        cols = slice((2 + i) * WIDTH, (3 + i) * WIDTH)
        g = nn(mine_ref[0], left_ref[i]) + nn(other_ref[0], right_ref[i])
        own_ref[:, cols] = g[:128]
        for k in range(3):
            sent[k][:, cols] = g[(k + 1) * 128 : (k + 2) * 128].astype(BF)


def ysum_kernel(own_ref, r1_ref, r2_ref, r3_ref, kept_ref, *sent):
    total = own_ref[...]
    for r in (r1_ref, r2_ref, r3_ref):
        total = total + r[...].astype(F32)
    kept_ref[...] = total[:32]
    for m in range(3):
        sent[m][...] = total[32 * m + 32 : 32 * m + 64].astype(BF)


def sum_kernel(*refs):
    *parts, out_ref = refs
    total = parts[0][...].astype(F32)
    for r in parts[1:]:
        total = total + r[...].astype(F32)
    out_ref[...] = total.astype(BF)


def join_kernel(*refs, order):
    *parts, out_ref = refs
    rows = parts[0].shape[0]
    for i, r in zip(order, parts):
        out_ref[i * rows : (i + 1) * rows, :] = r[...]


def place_kernel(*refs):
    mine, other, (qkv_ref, out_ref, held, turned, sems) = refs[:4], refs[4:8], refs[8:]
    z, core, y, _ = place_of()
    copies = []
    for n, k in enumerate(PLACE_ORDER):
        block = pl.ds(pl.multiple_of((y ^ k) * 256, 256), 256)
        for array, column in ((3, 1), (0, 0), (1, 2), (2, 3)):
            cols = slice(column * WIDTH, (column + 1) * WIDTH)
            for side, blocks in ((core, mine), (1 - core, other)):
                for m in range(4):
                    rows = pl.ds(pl.multiple_of(side * 128 + ((z & 3) ^ m) * 32, 32), 32)
                    held[k, array, rows, :] = blocks[n][m * 32 : m * 32 + 32, cols].astype(F32)
            if array == 3:
                turned[k] = held[k, 3].T
                copy = pltpu.make_async_copy(turned.at[k], out_ref.at[:, block], sems.at[k, 3])
            else:
                copy = pltpu.make_async_copy(
                    held.at[k, array], qkv_ref.at[array, block], sems.at[k, array]
                )
            copy.start()
            copies.append(copy)
    for copy in copies:
        copy.wait()


def per_device(tokens, neighbours, counts, w_qkv, w_out, cotangent):
    x, listed, occupied, cot = tokens[0], neighbours[0], counts[0], cotangent[0]
    n = 16
    swap = [(i, i ^ 1) for i in range(n)]
    cross = [(i, i if i in (0, n - 1) else i + 1 if i % 2 else i - 1) for i in range(n)]

    def pair_z(k):
        return [(i, i ^ (2 * k)) for i in range(n)]

    def pair(k):
        return [(i, i ^ k) for i in range(4)]

    def swapped(a):
        return lax.ppermute(a, "spatial", swap)

    kv = call(
        kv_kernel,
        [shape((2, ROWS, WIDTH), BF)],
        [x, w_qkv],
        4 * ROWS * D * WIDTH,
        [HBM] * 2,
        scratch=[
            pltpu.VMEM((ROWS, D), BF),
            pltpu.VMEM((2, D, WIDTH), BF),
            pltpu.SemaphoreType.DMA((3,)),
        ],
        vmem=53.5,
    )[0]
    blocks = jnp.concatenate(
        [
            jnp.pad(listed, ((0, 0), (0, 128 - listed.shape[1])), constant_values=-1),
            jnp.pad(occupied[None], ((0, 0), (0, 128 - occupied.shape[0]))),
        ],
        axis=0,
    )
    q, u, xc_sent, bias = call(
        prep_kernel,
        [shape((ROWS, WIDTH), BF)] * 2 + [shape((2, 512, ROWS), BF), shape((4, 12 * BLOCK), F32)],
        [x, w_qkv, w_out, cot, blocks],
        8 * ROWS * D * WIDTH,
        [HBM] * 4 + [VMEM],
        scratch=[
            pltpu.VMEM((ROWS, D), BF),
            pltpu.VMEM((D, WIDTH), BF),
            pltpu.VMEM((WIDTH, D), BF),
            pltpu.VMEM((ROWS, D), BF),
            pltpu.SemaphoreType.DMA((4,)),
        ],
        vmem=53,
        after=[kv],
    )
    mate_kv = swapped(kv)
    far_kv = lax.ppermute(kv, "spatial", cross)

    xc_other = swapped(xc_sent)

    acts, grad_far, grad_own, grad_mate = call(
        attention_kernel,
        [
            shape((2, ROWS, WIDTH), BF),
            shape((2, ROWS, WIDTH), BF),
            shape((2, ROWS, WIDTH), F32),
            shape((2, ROWS, WIDTH), BF),
        ],
        [q, u, mate_kv, kv, far_kv, bias],
        10 * 256 * 768 * 256,
        vmem=32,
    )
    from_far = lax.ppermute(grad_far, "spatial", cross)
    from_mate = swapped(grad_mate)
    acts_other = swapped(acts)
    xc_mine = call(
        mine_kernel,
        [shape((2, 512, ROWS), BF)],
        [x, cot],
        4 * 512 * 256 * D,
        after=[acts],
    )[0]
    early = call(
        early_kernel,
        [shape((128, 512), F32), shape((384, 512), BF)],
        [xc_mine, xc_other, acts, acts_other],
        4 * 512 * 512 * 256,
    )
    dkv = call(
        dkv_kernel,
        [shape((2, ROWS, WIDTH), BF)],
        [grad_own, from_far, from_mate],
        2**18,
        after=[early[0]],
    )[0]
    own, *to_y = call(
        late_kernel,
        [shape((128, D), F32)] + [shape((128, D), BF)] * 3,
        [xc_mine, xc_other, dkv, swapped(dkv), *early],
        4 * 512 * 512 * 256,
    )
    from_y = [lax.ppermute(to_y[k - 1], "dp", pair(k)) for k in (1, 3, 2)]

    head_own, *to_head = call(
        functools.partial(head_kernel, parts=(0, 1, 3)),
        [shape((2, ROWS, WIDTH), F32)] + [shape((2, ROWS, WIDTH), BF)] * 2,
        [acts, dkv, w_out, w_qkv],
        6 * ROWS * WIDTH * D,
        after=[own],
    )
    from_head = [lax.ppermute(a, "head", pair(k)) for k, a in zip((1, 3), to_head)]

    own, *to_z = call(
        ysum_kernel,
        [shape((32, D), F32)] + [shape((32, D), BF)] * 3,
        [own] + from_y,
        2**20,
    )
    from_z = [lax.ppermute(to_z[m - 1], "spatial", pair_z(m)) for m in (2, 3, 1)]
    part = call(sum_kernel, [shape((32, D), BF)], [own] + from_z, 2**18)[0]
    far_part = lax.ppermute(part, "spatial", pair_z(4))
    chunk = call(sum_kernel, [shape((32, D), BF)], [part, far_part], 2**16)[0]
    pieces = [chunk] + [lax.ppermute(chunk, "spatial", pair_z(m)) for m in (1, 3, 2)]
    column = call(
        functools.partial(join_kernel, order=(0, 1, 3, 2)),
        [shape((128, D), BF)],
        pieces,
        2**16,
        after=from_head,
    )[0]
    mine = [column] + [lax.ppermute(column, "dp", pair(k)) for k in PLACE_ORDER[1:]]
    last = call(
        functools.partial(head_kernel, parts=(2,)),
        [shape((2, ROWS, WIDTH), BF)],
        [acts, dkv, w_out, w_qkv],
        2 * ROWS * WIDTH * D,
        after=[column],
    )[0]
    from_head.append(lax.ppermute(last, "head", pair(2)))
    layer_out, grad_tokens, token = call(
        head_sum_kernel,
        [shape((ROWS, WIDTH), BF)] * 2 + [shape((8, 128), F32)],
        [head_own, *from_head, x, cot],
        2**20,
    )
    other = [swapped(a) for a in mine]
    grad_qkv, grad_out = call(
        place_kernel,
        [shape((3, D, WIDTH), F32), shape((WIDTH, D), F32)],
        mine + other,
        2**20,
        scratch=[
            pltpu.VMEM((4, 4, 256, WIDTH), F32),
            pltpu.VMEM((4, WIDTH, 256), F32),
            pltpu.SemaphoreType.DMA((4, 4)),
        ],
        out_specs=[ANY, ANY],
        after=[token],
    )
    return layer_out[None], grad_tokens[None], grad_qkv, grad_out


def solution(mesh):
    in_specs = (
        P("dp", "spatial", None),
        P("dp", "spatial", None),
        P("dp", None),
        P(None, None, "head"),
        P("head", None),
        P("dp", "spatial", None),
    )
    out_specs = (
        P("dp", "spatial", "head"),
        P("dp", "spatial", "head"),
        P(None, None, "head"),
        P("head", None),
    )
    return jax.shard_map(
        per_device, mesh=mesh, in_specs=in_specs, out_specs=out_specs, check_vma=False
    )
```

```python
import functools

import jax
import jax.numpy as jnp
from jax import lax
from jax.experimental import pallas as pl
from jax.experimental.pallas import tpu as pltpu
from jax.sharding import PartitionSpec as P

HD = 64
BLOCK = 64
ROWS = 256
WIDTH = 256
D = 1024
PLACE_ORDER = (0, 2, 3, 1)
LOG2E = 1.4426950408889634
BF = jnp.bfloat16
F32 = jnp.float32
VMEM = pl.BlockSpec(memory_space=pltpu.VMEM)
ANY = pl.BlockSpec(memory_space=pl.ANY)
HBM = pl.BlockSpec(memory_space=pltpu.HBM)


def call(kernel, outs, operands, flops, in_specs=None, scratch=(), vmem=24, after=(), out_specs=None):
    moved = sum(a.size * a.dtype.itemsize for a in operands)
    moved += sum(o.size * o.dtype.itemsize for o in outs)
    count = len(operands)

    def body(*refs):
        kernel(*refs[:count], *refs[count + len(after) :])

    return pl.pallas_call(
        body,
        out_shape=outs,
        in_specs=(in_specs or [VMEM] * count) + [ANY] * len(after),
        out_specs=out_specs or [VMEM] * len(outs),
        scratch_shapes=list(scratch),
        compiler_params=pltpu.CompilerParams(vmem_limit_bytes=int(vmem * 2**20)),
        cost_estimate=pl.CostEstimate(flops=flops, bytes_accessed=moved, transcendentals=0),
    )(*operands, *after)


def shape(dims, kind):
    return jax.ShapeDtypeStruct(dims, kind)


def nn(a, b):
    return lax.dot_general(a, b, (((1,), (0,)), ((), ())), preferred_element_type=F32)


def nt(a, b):
    return lax.dot_general(a, b, (((1,), (1,)), ((), ())), preferred_element_type=F32)


def tn(a, b):
    return lax.dot_general(a, b, (((0,), (0,)), ((), ())), preferred_element_type=F32)


def place_of():
    spatial = lax.axis_index("spatial")
    return spatial >> 1, spatial & 1, lax.axis_index("dp"), lax.axis_index("head")


def picker(side):
    z, _, y, _ = place_of()
    c = lax.broadcasted_iota(jnp.int32, (512, 1), 0)
    k, m = c >> 7, (c >> 5) & 3
    row = (y ^ k) * 256 + side * 128 + ((z & 3) ^ m) * 32 + (c & 31)
    feature = lax.broadcasted_iota(jnp.int32, (512, D), 1)
    return (feature == row).astype(F32).astype(BF)


def pick_rows(side, x_ref, cot_ref, out_ref):
    pick = picker(side)
    out_ref[0] = nt(pick, x_ref[...]).astype(BF)
    out_ref[1] = nt(pick, cot_ref[...]).astype(BF)


def fetch(pairs, sems):
    loads = [pltpu.make_async_copy(a, b, sems.at[i]) for i, (a, b) in enumerate(pairs)]
    for load in loads:
        load.start()
    return loads


def kv_kernel(x_hbm, w_hbm, out_ref, x_ref, w_ref, sems):
    pairs = [(x_hbm, x_ref), (w_hbm.at[1], w_ref.at[0]), (w_hbm.at[2], w_ref.at[1])]
    x_load, *loads = fetch(pairs, sems)
    x_load.wait()
    for i in range(2):
        loads[i].wait()
        out_ref[i] = nn(x_ref[...], w_ref[i]).astype(BF)


def prep_kernel(
    x_hbm, w_hbm, wo_hbm, cot_hbm, blocks_ref,
    q_ref, u_ref, xc_ref, bias_ref, x_ref, w_ref, wo_ref, cot_ref, sems
):
    pairs = [(x_hbm, x_ref), (w_hbm.at[0], w_ref), (cot_hbm, cot_ref), (wo_hbm, wo_ref)]
    x_load, w_load, cot_load, wo_load = fetch(pairs, sems)

    z, core, _, _ = place_of()
    base = (z * 2 + core) * 4
    starts = (base - 4 + 8 * core, base, base + 4 - 8 * core)
    lane = lax.broadcasted_iota(jnp.int32, (4, 128), 1)
    slot = (lane & (BLOCK - 1)).astype(F32)
    table = lax.broadcasted_iota(jnp.int32, (1, 128), 1)
    listed, occupied = blocks_ref[0:4, :], blocks_ref[4:5, :].astype(F32)

    def limit(block):
        hit = jnp.max(jnp.where(listed == block, 1.0, 0.0), axis=1, keepdims=True)
        return hit * jnp.sum(jnp.where(table == block, occupied, 0.0), axis=1, keepdims=True)

    for w in range(0, 12, 2):
        block = starts[w // 4] + w % 4
        edge = jnp.where(lane < BLOCK, limit(block), limit(block + 1))
        bias_ref[:, w * BLOCK : (w + 2) * BLOCK] = jnp.where(slot < edge, 0.0, -1e30)

    x_load.wait()
    w_load.wait()
    q_ref[...] = nn(x_ref[...], w_ref[...]).astype(BF)
    cot_load.wait()
    wo_load.wait()
    u_ref[...] = nt(cot_ref[...], wo_ref[...]).astype(BF)
    pick_rows(1 - core, x_ref, cot_ref, xc_ref)


def mine_kernel(x_ref, cot_ref, xc_ref):
    pick_rows(place_of()[1], x_ref, cot_ref, xc_ref)


def attention_kernel(q_ref, u_ref, mate_ref, own_ref, far_ref, bias_ref, acts_ref, gf_ref, go_ref, gm_ref):
    factor = HD**-0.5
    window = (far_ref, own_ref, mate_ref)
    grads = (gf_ref, go_ref, gm_ref)
    lane = lax.broadcasted_iota(jnp.int32, (1, 128), 1)
    picks = [(lane < HD).astype(F32).astype(BF), (lane >= HD).astype(F32).astype(BF)]
    first = lax.broadcasted_iota(jnp.int32, (ROWS, 128), 1) < HD
    bias = [
        jnp.concatenate(
            [
                jnp.broadcast_to(bias_ref[b : b + 1, c * ROWS : (c + 1) * ROWS], (BLOCK, ROWS))
                for b in range(ROWS // BLOCK)
            ],
            axis=0,
        )
        for c in range(3)
    ]
    for pair in range(WIDTH // 128):
        cols = slice(pair * 128, (pair + 1) * 128)
        q2, u2 = q_ref[:, cols], u_ref[:, cols]
        keys = [w[0, :, cols] for w in window]
        values = [w[1, :, cols] for w in window]
        key_sum, value_sum = [None] * 3, [None] * 3
        att, dq = [], []
        for pick in picks:
            qm, um = q2 * pick, u2 * pick
            weights = [jnp.exp2(nt(qm, keys[c]) * (factor * LOG2E) + bias[c]) for c in range(3)]
            total = sum(jnp.sum(w, axis=1, keepdims=True) for w in weights)
            share = 1.0 / total
            probs = [w * share for w in weights]
            low = [p.astype(BF) for p in probs]
            dprob = [nt(um, values[c]) for c in range(3)]
            spread = sum(jnp.sum(p * d, axis=1, keepdims=True) for p, d in zip(probs, dprob))
            dscore = [(p * (d - spread) * factor).astype(BF) for p, d in zip(probs, dprob)]
            att.append(sum(nn(low[c], values[c]) for c in range(3)))
            dq.append(sum(nn(dscore[c], keys[c]) for c in range(3)))
            for c in range(3):
                dk, dv = tn(dscore[c], qm), tn(low[c], um)
                key_sum[c] = dk if key_sum[c] is None else key_sum[c] + dk
                value_sum[c] = dv if value_sum[c] is None else value_sum[c] + dv
        acts_ref[0, :, cols] = jnp.where(first, att[0], att[1]).astype(BF)
        acts_ref[1, :, cols] = jnp.where(first, dq[0], dq[1]).astype(BF)
        for c in range(3):
            grads[c][0, :, cols] = key_sum[c].astype(grads[c].dtype)
            grads[c][1, :, cols] = value_sum[c].astype(grads[c].dtype)


def head_kernel(acts_ref, dkv_ref, wo_ref, w_ref, *outs, parts):
    head = place_of()[3]
    for to, k in zip(outs, parts):
        span = pl.ds(pl.multiple_of((head ^ k) * WIDTH, WIDTH), WIDTH)
        out = nn(acts_ref[0], wo_ref[:, span])
        grad = nt(acts_ref[1], w_ref[0, span, :])
        grad = grad + nt(dkv_ref[0], w_ref[1, span, :])
        grad = grad + nt(dkv_ref[1], w_ref[2, span, :])
        to[0] = out.astype(to.dtype)
        to[1] = grad.astype(to.dtype)


def head_sum_kernel(own_ref, r1_ref, r2_ref, r3_ref, x_ref, cot_ref, out_ref, grad_ref, token_ref):
    token_ref[...] = jnp.zeros_like(token_ref)
    span = pl.ds(pl.multiple_of(place_of()[3] * WIDTH, WIDTH), WIDTH)
    for i, (base, to) in enumerate(((x_ref, out_ref), (cot_ref, grad_ref))):
        total = own_ref[i] + r1_ref[i].astype(F32) + r2_ref[i].astype(F32) + r3_ref[i].astype(F32)
        to[...] = (base[:, span].astype(F32) + total).astype(BF)


def dkv_kernel(own_ref, a_ref, b_ref, out_ref):
    out_ref[...] = (own_ref[...] + a_ref[...].astype(F32) + b_ref[...].astype(F32)).astype(BF)


def early_kernel(mine_ref, other_ref, left_ref, right_ref, own_ref, rest_ref):
    for i, (side, act) in enumerate(((0, 1), (1, 0))):
        cols = slice(i * WIDTH, (i + 1) * WIDTH)
        g = nn(mine_ref[side], left_ref[act]) + nn(other_ref[side], right_ref[act])
        own_ref[:, cols] = g[:128]
        rest_ref[:, cols] = g[128:].astype(BF)


def late_kernel(mine_ref, other_ref, left_ref, right_ref, own1_ref, rest1_ref, own_ref, *sent):
    own_ref[:, : 2 * WIDTH] = own1_ref[...]
    for k in range(3):
        sent[k][:, : 2 * WIDTH] = rest1_ref[k * 128 : (k + 1) * 128, :]
    for i in range(2):
        cols = slice((2 + i) * WIDTH, (3 + i) * WIDTH)
        g = nn(mine_ref[0], left_ref[i]) + nn(other_ref[0], right_ref[i])
        own_ref[:, cols] = g[:128]
        for k in range(3):
            sent[k][:, cols] = g[(k + 1) * 128 : (k + 2) * 128].astype(BF)


def ysum_kernel(own_ref, r1_ref, r2_ref, r3_ref, kept_ref, *sent):
    total = own_ref[...]
    for r in (r1_ref, r2_ref, r3_ref):
        total = total + r[...].astype(F32)
    kept_ref[...] = total[:32]
    for m in range(3):
        sent[m][...] = total[32 * m + 32 : 32 * m + 64].astype(BF)


def sum_kernel(*refs):
    *parts, out_ref = refs
    total = parts[0][...].astype(F32)
    for r in parts[1:]:
        total = total + r[...].astype(F32)
    out_ref[...] = total.astype(BF)


def join_kernel(*refs, order):
    *parts, out_ref = refs
    rows = parts[0].shape[0]
    for i, r in zip(order, parts):
        out_ref[i * rows : (i + 1) * rows, :] = r[...]


def place_kernel(*refs):
    mine, other, (qkv_ref, out_ref, held, turned, sems) = refs[:4], refs[4:8], refs[8:]
    z, core, y, _ = place_of()
    copies = []
    for n, k in enumerate(PLACE_ORDER):
        block = pl.ds(pl.multiple_of((y ^ k) * 256, 256), 256)
        for array, column in ((3, 1), (0, 0), (1, 2), (2, 3)):
            cols = slice(column * WIDTH, (column + 1) * WIDTH)
            for side, blocks in ((core, mine), (1 - core, other)):
                for m in range(4):
                    rows = pl.ds(pl.multiple_of(side * 128 + ((z & 3) ^ m) * 32, 32), 32)
                    held[k, array, rows, :] = blocks[n][m * 32 : m * 32 + 32, cols].astype(F32)
            if array == 3:
                turned[k] = held[k, 3].T
                copy = pltpu.make_async_copy(turned.at[k], out_ref.at[:, block], sems.at[k, 3])
            else:
                copy = pltpu.make_async_copy(
                    held.at[k, array], qkv_ref.at[array, block], sems.at[k, array]
                )
            copy.start()
            copies.append(copy)
    for copy in copies:
        copy.wait()


def per_device(tokens, neighbours, counts, w_qkv, w_out, cotangent):
    x, listed, occupied, cot = tokens[0], neighbours[0], counts[0], cotangent[0]
    n = 16
    swap = [(i, i ^ 1) for i in range(n)]
    cross = [(i, (i + 1) % n if i % 2 else (i - 1) % n) for i in range(n)]

    def pair_z(k):
        return [(i, i ^ (2 * k)) for i in range(n)]

    def pair(k):
        return [(i, i ^ k) for i in range(4)]

    def swapped(a):
        return lax.ppermute(a, "spatial", swap)

    kv = call(
        kv_kernel,
        [shape((2, ROWS, WIDTH), BF)],
        [x, w_qkv],
        4 * ROWS * D * WIDTH,
        [HBM] * 2,
        scratch=[
            pltpu.VMEM((ROWS, D), BF),
            pltpu.VMEM((2, D, WIDTH), BF),
            pltpu.SemaphoreType.DMA((3,)),
        ],
        vmem=53.5,
    )[0]
    blocks = jnp.concatenate(
        [
            jnp.pad(listed, ((0, 0), (0, 128 - listed.shape[1])), constant_values=-1),
            jnp.pad(occupied[None], ((0, 0), (0, 128 - occupied.shape[0]))),
        ],
        axis=0,
    )
    q, u, xc_sent, bias = call(
        prep_kernel,
        [shape((ROWS, WIDTH), BF)] * 2 + [shape((2, 512, ROWS), BF), shape((4, 12 * BLOCK), F32)],
        [x, w_qkv, w_out, cot, blocks],
        8 * ROWS * D * WIDTH,
        [HBM] * 4 + [VMEM],
        scratch=[
            pltpu.VMEM((ROWS, D), BF),
            pltpu.VMEM((D, WIDTH), BF),
            pltpu.VMEM((WIDTH, D), BF),
            pltpu.VMEM((ROWS, D), BF),
            pltpu.SemaphoreType.DMA((4,)),
        ],
        vmem=53,
        after=[kv],
    )
    mate_kv = swapped(kv)
    far_kv = lax.ppermute(kv, "spatial", cross)

    xc_other = swapped(xc_sent)

    acts, grad_far, grad_own, grad_mate = call(
        attention_kernel,
        [
            shape((2, ROWS, WIDTH), BF),
            shape((2, ROWS, WIDTH), BF),
            shape((2, ROWS, WIDTH), F32),
            shape((2, ROWS, WIDTH), BF),
        ],
        [q, u, mate_kv, kv, far_kv, bias],
        10 * 256 * 768 * 256,
        vmem=32,
    )
    from_far = lax.ppermute(grad_far, "spatial", cross)
    from_mate = swapped(grad_mate)
    acts_other = swapped(acts)
    xc_mine = call(
        mine_kernel,
        [shape((2, 512, ROWS), BF)],
        [x, cot],
        4 * 512 * 256 * D,
        after=[acts],
    )[0]
    early = call(
        early_kernel,
        [shape((128, 512), F32), shape((384, 512), BF)],
        [xc_mine, xc_other, acts, acts_other],
        4 * 512 * 512 * 256,
    )
    dkv = call(
        dkv_kernel,
        [shape((2, ROWS, WIDTH), BF)],
        [grad_own, from_far, from_mate],
        2**18,
        after=[early[0]],
    )[0]
    own, *to_y = call(
        late_kernel,
        [shape((128, D), F32)] + [shape((128, D), BF)] * 3,
        [xc_mine, xc_other, dkv, swapped(dkv), *early],
        4 * 512 * 512 * 256,
    )
    from_y = [lax.ppermute(to_y[k - 1], "dp", pair(k)) for k in (1, 3, 2)]

    head_own, *to_head = call(
        functools.partial(head_kernel, parts=(0, 1, 3)),
        [shape((2, ROWS, WIDTH), F32)] + [shape((2, ROWS, WIDTH), BF)] * 2,
        [acts, dkv, w_out, w_qkv],
        6 * ROWS * WIDTH * D,
        after=[own],
    )
    from_head = [lax.ppermute(a, "head", pair(k)) for k, a in zip((1, 3), to_head)]

    own, *to_z = call(
        ysum_kernel,
        [shape((32, D), F32)] + [shape((32, D), BF)] * 3,
        [own] + from_y,
        2**20,
    )
    from_z = [lax.ppermute(to_z[m - 1], "spatial", pair_z(m)) for m in (2, 3, 1)]
    part = call(sum_kernel, [shape((32, D), BF)], [own] + from_z, 2**18)[0]
    far_part = lax.ppermute(part, "spatial", pair_z(4))
    chunk = call(sum_kernel, [shape((32, D), BF)], [part, far_part], 2**16)[0]
    pieces = [chunk] + [lax.ppermute(chunk, "spatial", pair_z(m)) for m in (1, 3, 2)]
    column = call(
        functools.partial(join_kernel, order=(0, 1, 3, 2)),
        [shape((128, D), BF)],
        pieces,
        2**16,
        after=from_head,
    )[0]
    mine = [column] + [lax.ppermute(column, "dp", pair(k)) for k in PLACE_ORDER[1:]]
    last = call(
        functools.partial(head_kernel, parts=(2,)),
        [shape((2, ROWS, WIDTH), BF)],
        [acts, dkv, w_out, w_qkv],
        2 * ROWS * WIDTH * D,
        after=[column],
    )[0]
    from_head.append(lax.ppermute(last, "head", pair(2)))
    layer_out, grad_tokens, token = call(
        head_sum_kernel,
        [shape((ROWS, WIDTH), BF)] * 2 + [shape((8, 128), F32)],
        [head_own, *from_head, x, cot],
        2**20,
    )
    other = [swapped(a) for a in mine]
    grad_qkv, grad_out = call(
        place_kernel,
        [shape((3, D, WIDTH), F32), shape((WIDTH, D), F32)],
        mine + other,
        2**20,
        scratch=[
            pltpu.VMEM((4, 4, 256, WIDTH), F32),
            pltpu.VMEM((4, WIDTH, 256), F32),
            pltpu.SemaphoreType.DMA((4, 4)),
        ],
        out_specs=[ANY, ANY],
        after=[token],
    )
    return layer_out[None], grad_tokens[None], grad_qkv, grad_out


def solution(mesh):
    in_specs = (
        P("dp", "spatial", None),
        P("dp", "spatial", None),
        P("dp", None),
        P(None, None, "head"),
        P("head", None),
        P("dp", "spatial", None),
    )
    out_specs = (
        P("dp", "spatial", "head"),
        P("dp", "spatial", "head"),
        P(None, None, "head"),
        P("head", None),
    )
    return jax.shard_map(
        per_device, mesh=mesh, in_specs=in_specs, out_specs=out_specs, check_vma=False
    )
```

```python
import functools

import jax
import jax.numpy as jnp
from jax import lax
from jax.experimental import pallas as pl
from jax.experimental.pallas import tpu as pltpu
from jax.sharding import PartitionSpec as P

HD = 64
BLOCK = 64
ROWS = 256
WIDTH = 256
D = 1024
PLACE_ORDER = (0, 2, 3, 1)
LOG2E = 1.4426950408889634
BF = jnp.bfloat16
F32 = jnp.float32
VMEM = pl.BlockSpec(memory_space=pltpu.VMEM)
ANY = pl.BlockSpec(memory_space=pl.ANY)
HBM = pl.BlockSpec(memory_space=pltpu.HBM)


def call(kernel, outs, operands, flops, in_specs=None, scratch=(), vmem=24, after=(), out_specs=None):
    moved = sum(a.size * a.dtype.itemsize for a in operands)
    moved += sum(o.size * o.dtype.itemsize for o in outs)
    count = len(operands)

    def body(*refs):
        kernel(*refs[:count], *refs[count + len(after) :])

    return pl.pallas_call(
        body,
        out_shape=outs,
        in_specs=(in_specs or [VMEM] * count) + [ANY] * len(after),
        out_specs=out_specs or [VMEM] * len(outs),
        scratch_shapes=list(scratch),
        compiler_params=pltpu.CompilerParams(vmem_limit_bytes=int(vmem * 2**20)),
        cost_estimate=pl.CostEstimate(flops=flops, bytes_accessed=moved, transcendentals=0),
    )(*operands, *after)


def shape(dims, kind):
    return jax.ShapeDtypeStruct(dims, kind)


def nn(a, b):
    return lax.dot_general(a, b, (((1,), (0,)), ((), ())), preferred_element_type=F32)


def nt(a, b):
    return lax.dot_general(a, b, (((1,), (1,)), ((), ())), preferred_element_type=F32)


def place_of():
    spatial = lax.axis_index("spatial")
    return spatial >> 1, spatial & 1, lax.axis_index("dp"), lax.axis_index("head")


def picker(side):
    z, _, y, _ = place_of()
    c = lax.broadcasted_iota(jnp.int32, (512, 1), 0)
    k, m = c >> 7, (c >> 5) & 3
    row = (y ^ k) * 256 + side * 128 + ((z & 3) ^ m) * 32 + (c & 31)
    feature = lax.broadcasted_iota(jnp.int32, (512, D), 1)
    return (feature == row).astype(F32).astype(BF)


def pick_rows(side, x_ref, cot_ref, out_ref):
    pick = picker(side)
    out_ref[0] = nt(pick, x_ref[...]).astype(BF)
    out_ref[1] = nt(pick, cot_ref[...]).astype(BF)


def fetch(pairs, sems):
    loads = [pltpu.make_async_copy(a, b, sems.at[i]) for i, (a, b) in enumerate(pairs)]
    for load in loads:
        load.start()
    return loads


def kv_kernel(x_hbm, w_hbm, out_ref, x_ref, w_ref, sems):
    pairs = [(x_hbm, x_ref), (w_hbm.at[1], w_ref.at[0]), (w_hbm.at[2], w_ref.at[1])]
    x_load, *loads = fetch(pairs, sems)
    x_load.wait()
    for i in range(2):
        loads[i].wait()
        out_ref[i] = nn(x_ref[...], w_ref[i]).astype(BF)


def prep_kernel(
    x_hbm, w_hbm, wo_hbm, cot_hbm, blocks_ref,
    q_ref, u_ref, xc_ref, bias_ref, x_ref, w_ref, wo_ref, cot_ref, sems
):
    pairs = [(x_hbm, x_ref), (w_hbm.at[0], w_ref), (cot_hbm, cot_ref), (wo_hbm, wo_ref)]
    x_load, w_load, cot_load, wo_load = fetch(pairs, sems)

    z, core, _, _ = place_of()
    base = (z * 2 + core) * 4
    starts = (base - 4 + 8 * core, base, base + 4 - 8 * core)
    lane = lax.broadcasted_iota(jnp.int32, (4, 128), 1)
    slot = (lane & (BLOCK - 1)).astype(F32)
    table = lax.broadcasted_iota(jnp.int32, (1, 128), 1)
    listed, occupied = blocks_ref[0:4, :], blocks_ref[4:5, :].astype(F32)

    def limit(block):
        hit = jnp.max(jnp.where(listed == block, 1.0, 0.0), axis=1, keepdims=True)
        return hit * jnp.sum(jnp.where(table == block, occupied, 0.0), axis=1, keepdims=True)

    for w in range(0, 12, 2):
        block = starts[w // 4] + w % 4
        edge = jnp.where(lane < BLOCK, limit(block), limit(block + 1))
        bias_ref[:, w * BLOCK : (w + 2) * BLOCK] = jnp.where(slot < edge, 0.0, -1e30)

    x_load.wait()
    w_load.wait()
    q_ref[...] = nn(x_ref[...], w_ref[...]).astype(BF)
    cot_load.wait()
    wo_load.wait()
    u_ref[...] = nt(cot_ref[...], wo_ref[...]).astype(BF)
    pick_rows(1 - core, x_ref, cot_ref, xc_ref)


def mine_kernel(x_ref, cot_ref, xc_ref):
    pick_rows(place_of()[1], x_ref, cot_ref, xc_ref)


def attention_kernel(q_ref, u_ref, mate_ref, own_ref, far_ref, bias_ref, acts_ref, gf_ref, go_ref):
    factor = HD**-0.5
    window = (far_ref, own_ref, mate_ref)
    grads = (gf_ref, go_ref, acts_ref.at[2:4])
    lane = lax.broadcasted_iota(jnp.int32, (1, 128), 1)
    picks = [(lane < HD).astype(F32).astype(BF), (lane >= HD).astype(F32).astype(BF)]
    first = lax.broadcasted_iota(jnp.int32, (ROWS, 128), 1) < HD
    bias = [
        jnp.concatenate(
            [
                jnp.broadcast_to(bias_ref[b : b + 1, c * ROWS : (c + 1) * ROWS], (BLOCK, ROWS))
                for b in range(ROWS // BLOCK)
            ],
            axis=0,
        )
        for c in range(3)
    ]
    for pair in range(WIDTH // 128):
        cols = slice(pair * 128, (pair + 1) * 128)
        q2, u2 = q_ref[:, cols], u_ref[:, cols]
        q_turned, u_turned = q2.T, u2.T
        keys = [w[0, :, cols] for w in window]
        values = [w[1, :, cols] for w in window]
        key_parts, value_parts = [[], [], []], [[], [], []]
        att, dq = [], []
        for h, pick in enumerate(picks):
            rows = slice(h * HD, (h + 1) * HD)
            qm, um = q2 * pick, u2 * pick
            weights = [jnp.exp2(nt(qm, keys[c]) * (factor * LOG2E) + bias[c]) for c in range(3)]
            total = sum(jnp.sum(w, axis=1, keepdims=True) for w in weights)
            share = 1.0 / total
            probs = [w * share for w in weights]
            low = [p.astype(BF) for p in probs]
            dprob = [nt(um, values[c]) for c in range(3)]
            spread = sum(jnp.sum(p * d, axis=1, keepdims=True) for p, d in zip(probs, dprob))
            dscore = [(p * (d - spread) * factor).astype(BF) for p, d in zip(probs, dprob)]
            att.append(sum(nn(low[c], values[c]) for c in range(3)))
            dq.append(sum(nn(dscore[c], keys[c]) for c in range(3)))
            for c in range(3):
                key_parts[c].append(nn(q_turned[rows], dscore[c]))
                value_parts[c].append(nn(u_turned[rows], low[c]))
        acts_ref[0, :, cols] = jnp.where(first, att[0], att[1]).astype(BF)
        acts_ref[1, :, cols] = jnp.where(first, dq[0], dq[1]).astype(BF)
        for c in range(3):
            grads[c][0, :, cols] = jnp.concatenate(key_parts[c], axis=0).T.astype(grads[c].dtype)
            grads[c][1, :, cols] = jnp.concatenate(value_parts[c], axis=0).T.astype(grads[c].dtype)


def head_kernel(acts_ref, dkv_ref, wo_ref, w_ref, *outs, parts):
    head = place_of()[3]
    for to, k in zip(outs, parts):
        span = pl.ds(pl.multiple_of((head ^ k) * WIDTH, WIDTH), WIDTH)
        out = nn(acts_ref[0], wo_ref[:, span])
        grad = nt(acts_ref[1], w_ref[0, span, :])
        grad = grad + nt(dkv_ref[0], w_ref[1, span, :])
        grad = grad + nt(dkv_ref[1], w_ref[2, span, :])
        to[0] = out.astype(to.dtype)
        to[1] = grad.astype(to.dtype)


def head_sum_kernel(own_ref, r1_ref, r2_ref, r3_ref, x_ref, cot_ref, out_ref, grad_ref, token_ref):
    token_ref[...] = jnp.zeros_like(token_ref)
    span = pl.ds(pl.multiple_of(place_of()[3] * WIDTH, WIDTH), WIDTH)
    for i, (base, to) in enumerate(((x_ref, out_ref), (cot_ref, grad_ref))):
        total = own_ref[i] + r1_ref[i].astype(F32) + r2_ref[i].astype(F32) + r3_ref[i].astype(F32)
        to[...] = (base[:, span].astype(F32) + total).astype(BF)


def dkv_kernel(own_ref, a_ref, b_ref, out_ref):
    out_ref[...] = (own_ref[...] + a_ref[...].astype(F32) + b_ref[2:4].astype(F32)).astype(BF)


def early_kernel(mine_ref, other_ref, left_ref, right_ref, own_ref, rest_ref):
    for i, (side, act) in enumerate(((0, 1), (1, 0))):
        cols = slice(i * WIDTH, (i + 1) * WIDTH)
        g = nn(mine_ref[side], left_ref[act]) + nn(other_ref[side], right_ref[act])
        own_ref[:, cols] = g[:128]
        rest_ref[:, cols] = g[128:].astype(BF)


def late_kernel(mine_ref, other_ref, left_ref, right_ref, own1_ref, rest1_ref, own_ref, *sent):
    own_ref[:, : 2 * WIDTH] = own1_ref[...]
    for k in range(3):
        sent[k][:, : 2 * WIDTH] = rest1_ref[k * 128 : (k + 1) * 128, :]
    for i in range(2):
        cols = slice((2 + i) * WIDTH, (3 + i) * WIDTH)
        g = nn(mine_ref[0], left_ref[i]) + nn(other_ref[0], right_ref[i])
        own_ref[:, cols] = g[:128]
        for k in range(3):
            sent[k][:, cols] = g[(k + 1) * 128 : (k + 2) * 128].astype(BF)


def ysum_kernel(own_ref, r1_ref, r2_ref, r3_ref, kept_ref, *sent):
    total = own_ref[...]
    for r in (r1_ref, r2_ref, r3_ref):
        total = total + r[...].astype(F32)
    kept_ref[...] = total[:32]
    for m in range(3):
        sent[m][...] = total[32 * m + 32 : 32 * m + 64].astype(BF)


def sum_kernel(*refs):
    *parts, out_ref = refs
    total = parts[0][...].astype(F32)
    for r in parts[1:]:
        total = total + r[...].astype(F32)
    out_ref[...] = total.astype(BF)


def join_kernel(*refs, order):
    *parts, out_ref = refs
    rows = parts[0].shape[0]
    for i, r in zip(order, parts):
        out_ref[i * rows : (i + 1) * rows, :] = r[...]


def place_kernel(*refs):
    mine, other, (qkv_ref, out_ref, held, turned, sems) = refs[:4], refs[4:8], refs[8:]
    z, core, y, _ = place_of()
    copies = []
    for n, k in enumerate(PLACE_ORDER):
        block = pl.ds(pl.multiple_of((y ^ k) * 256, 256), 256)
        for array, column in ((3, 1), (0, 0), (1, 2), (2, 3)):
            cols = slice(column * WIDTH, (column + 1) * WIDTH)
            for side, blocks in ((core, mine), (1 - core, other)):
                for m in range(4):
                    rows = pl.ds(pl.multiple_of(side * 128 + ((z & 3) ^ m) * 32, 32), 32)
                    held[k, array, rows, :] = blocks[n][m * 32 : m * 32 + 32, cols].astype(F32)
            if array == 3:
                turned[k] = held[k, 3].T
                copy = pltpu.make_async_copy(turned.at[k], out_ref.at[:, block], sems.at[k, 3])
            else:
                copy = pltpu.make_async_copy(
                    held.at[k, array], qkv_ref.at[array, block], sems.at[k, array]
                )
            copy.start()
            copies.append(copy)
    for copy in copies:
        copy.wait()


def per_device(tokens, neighbours, counts, w_qkv, w_out, cotangent):
    x, listed, occupied, cot = tokens[0], neighbours[0], counts[0], cotangent[0]
    n = 16
    swap = [(i, i ^ 1) for i in range(n)]
    cross = [(i, (i + 1) % n if i % 2 else (i - 1) % n) for i in range(n)]

    def pair_z(k):
        return [(i, i ^ (2 * k)) for i in range(n)]

    def pair(k):
        return [(i, i ^ k) for i in range(4)]

    def swapped(a):
        return lax.ppermute(a, "spatial", swap)

    kv = call(
        kv_kernel,
        [shape((2, ROWS, WIDTH), BF)],
        [x, w_qkv],
        4 * ROWS * D * WIDTH,
        [HBM] * 2,
        scratch=[
            pltpu.VMEM((ROWS, D), BF),
            pltpu.VMEM((2, D, WIDTH), BF),
            pltpu.SemaphoreType.DMA((3,)),
        ],
        vmem=53.5,
    )[0]
    blocks = jnp.concatenate(
        [
            jnp.pad(listed, ((0, 0), (0, 128 - listed.shape[1])), constant_values=-1),
            jnp.pad(occupied[None], ((0, 0), (0, 128 - occupied.shape[0]))),
        ],
        axis=0,
    )
    q, u, xc_sent, bias = call(
        prep_kernel,
        [shape((ROWS, WIDTH), BF)] * 2 + [shape((2, 512, ROWS), BF), shape((4, 12 * BLOCK), F32)],
        [x, w_qkv, w_out, cot, blocks],
        8 * ROWS * D * WIDTH,
        [HBM] * 4 + [VMEM],
        scratch=[
            pltpu.VMEM((ROWS, D), BF),
            pltpu.VMEM((D, WIDTH), BF),
            pltpu.VMEM((WIDTH, D), BF),
            pltpu.VMEM((ROWS, D), BF),
            pltpu.SemaphoreType.DMA((4,)),
        ],
        vmem=53,
        after=[kv],
    )
    mate_kv = swapped(kv)
    far_kv = lax.ppermute(kv, "spatial", cross)

    xc_other = swapped(xc_sent)

    acts, grad_far, grad_own = call(
        attention_kernel,
        [
            shape((4, ROWS, WIDTH), BF),
            shape((2, ROWS, WIDTH), BF),
            shape((2, ROWS, WIDTH), F32),
        ],
        [q, u, mate_kv, kv, far_kv, bias],
        10 * 256 * 768 * 256,
        vmem=32,
    )
    from_far = lax.ppermute(grad_far, "spatial", cross)
    acts_other = swapped(acts)
    xc_mine = call(
        mine_kernel,
        [shape((2, 512, ROWS), BF)],
        [x, cot],
        4 * 512 * 256 * D,
        after=[acts],
    )[0]
    early = call(
        early_kernel,
        [shape((128, 512), F32), shape((384, 512), BF)],
        [xc_mine, xc_other, acts, acts_other],
        4 * 512 * 512 * 256,
    )
    dkv = call(
        dkv_kernel,
        [shape((2, ROWS, WIDTH), BF)],
        [grad_own, from_far, acts_other],
        2**18,
        after=[early[0]],
    )[0]
    own, *to_y = call(
        late_kernel,
        [shape((128, D), F32)] + [shape((128, D), BF)] * 3,
        [xc_mine, xc_other, dkv, swapped(dkv), *early],
        4 * 512 * 512 * 256,
    )
    from_y = [lax.ppermute(to_y[k - 1], "dp", pair(k)) for k in (1, 3, 2)]

    head_own, *to_head = call(
        functools.partial(head_kernel, parts=(0, 1, 3)),
        [shape((2, ROWS, WIDTH), F32)] + [shape((2, ROWS, WIDTH), BF)] * 2,
        [acts, dkv, w_out, w_qkv],
        6 * ROWS * WIDTH * D,
        after=[own],
    )
    from_head = [lax.ppermute(a, "head", pair(k)) for k, a in zip((1, 3), to_head)]

    own, *to_z = call(
        ysum_kernel,
        [shape((32, D), F32)] + [shape((32, D), BF)] * 3,
        [own] + from_y,
        2**20,
    )
    from_z = [lax.ppermute(to_z[m - 1], "spatial", pair_z(m)) for m in (2, 3, 1)]
    part = call(sum_kernel, [shape((32, D), BF)], [own] + from_z, 2**18)[0]
    far_part = lax.ppermute(part, "spatial", pair_z(4))
    chunk = call(sum_kernel, [shape((32, D), BF)], [part, far_part], 2**16)[0]
    pieces = [chunk] + [lax.ppermute(chunk, "spatial", pair_z(m)) for m in (1, 3, 2)]
    column = call(
        functools.partial(join_kernel, order=(0, 1, 3, 2)),
        [shape((128, D), BF)],
        pieces,
        2**16,
        after=from_head,
    )[0]
    mine = [column] + [lax.ppermute(column, "dp", pair(k)) for k in PLACE_ORDER[1:]]
    last = call(
        functools.partial(head_kernel, parts=(2,)),
        [shape((2, ROWS, WIDTH), BF)],
        [acts, dkv, w_out, w_qkv],
        2 * ROWS * WIDTH * D,
        after=[column],
    )[0]
    from_head.append(lax.ppermute(last, "head", pair(2)))
    layer_out, grad_tokens, token = call(
        head_sum_kernel,
        [shape((ROWS, WIDTH), BF)] * 2 + [shape((8, 128), F32)],
        [head_own, *from_head, x, cot],
        2**20,
    )
    other = [swapped(a) for a in mine]
    grad_qkv, grad_out = call(
        place_kernel,
        [shape((3, D, WIDTH), F32), shape((WIDTH, D), F32)],
        mine + other,
        2**20,
        scratch=[
            pltpu.VMEM((4, 4, 256, WIDTH), F32),
            pltpu.VMEM((4, WIDTH, 256), F32),
            pltpu.SemaphoreType.DMA((4, 4)),
        ],
        out_specs=[ANY, ANY],
        after=[token],
    )
    return layer_out[None], grad_tokens[None], grad_qkv, grad_out


def solution(mesh):
    in_specs = (
        P("dp", "spatial", None),
        P("dp", "spatial", None),
        P("dp", None),
        P(None, None, "head"),
        P("head", None),
        P("dp", "spatial", None),
    )
    out_specs = (
        P("dp", "spatial", "head"),
        P("dp", "spatial", "head"),
        P(None, None, "head"),
        P("head", None),
    )
    return jax.shard_map(
        per_device, mesh=mesh, in_specs=in_specs, out_specs=out_specs, check_vma=False
    )
```

```python
import functools

import jax
import jax.numpy as jnp
from jax import lax
from jax.experimental import pallas as pl
from jax.experimental.pallas import tpu as pltpu
from jax.sharding import PartitionSpec as P

HD = 64
BLOCK = 64
ROWS = 256
WIDTH = 256
D = 1024
PLACE_ORDER = (0, 2, 3, 1)
LOG2E = 1.4426950408889634
BF = jnp.bfloat16
F32 = jnp.float32
VMEM = pl.BlockSpec(memory_space=pltpu.VMEM)
ANY = pl.BlockSpec(memory_space=pl.ANY)
HBM = pl.BlockSpec(memory_space=pltpu.HBM)


def call(kernel, outs, operands, flops, in_specs=None, scratch=(), vmem=24, after=(), out_specs=None):
    moved = sum(a.size * a.dtype.itemsize for a in operands)
    moved += sum(o.size * o.dtype.itemsize for o in outs)
    count = len(operands)

    def body(*refs):
        kernel(*refs[:count], *refs[count + len(after) :])

    return pl.pallas_call(
        body,
        out_shape=outs,
        in_specs=(in_specs or [VMEM] * count) + [ANY] * len(after),
        out_specs=out_specs or [VMEM] * len(outs),
        scratch_shapes=list(scratch),
        compiler_params=pltpu.CompilerParams(vmem_limit_bytes=int(vmem * 2**20)),
        cost_estimate=pl.CostEstimate(flops=flops, bytes_accessed=moved, transcendentals=0),
    )(*operands, *after)


def shape(dims, kind):
    return jax.ShapeDtypeStruct(dims, kind)


def nn(a, b):
    return lax.dot_general(a, b, (((1,), (0,)), ((), ())), preferred_element_type=F32)


def nt(a, b):
    return lax.dot_general(a, b, (((1,), (1,)), ((), ())), preferred_element_type=F32)


def place_of():
    spatial = lax.axis_index("spatial")
    return spatial >> 1, spatial & 1, lax.axis_index("dp"), lax.axis_index("head")


def picker(side):
    z, _, y, _ = place_of()
    c = lax.broadcasted_iota(jnp.int32, (512, 1), 0)
    k, m = c >> 7, (c >> 5) & 3
    row = (y ^ k) * 256 + side * 128 + ((z & 3) ^ m) * 32 + (c & 31)
    feature = lax.broadcasted_iota(jnp.int32, (512, D), 1)
    return (feature == row).astype(F32).astype(BF)


def pick_rows(pick, x_ref, cot_ref, out_ref):
    out_ref[0] = nt(pick, x_ref[...]).astype(BF)
    out_ref[1] = nt(pick, cot_ref[...]).astype(BF)


def fetch(pairs, sems):
    loads = [pltpu.make_async_copy(a, b, sems.at[i]) for i, (a, b) in enumerate(pairs)]
    for load in loads:
        load.start()
    return loads


def kv_kernel(x_hbm, w_hbm, out_ref, x_ref, w_ref, sems):
    pairs = [(x_hbm, x_ref), (w_hbm.at[1], w_ref.at[0]), (w_hbm.at[2], w_ref.at[1])]
    x_load, *loads = fetch(pairs, sems)
    x_load.wait()
    for i in range(2):
        loads[i].wait()
        out_ref[i] = nn(x_ref[...], w_ref[i]).astype(BF)


def prep_kernel(
    x_hbm, w_hbm, wo_hbm, cot_hbm, blocks_ref,
    q_ref, u_ref, xc_ref, bias_ref, x_ref, w_ref, wo_ref, cot_ref, sems
):
    pairs = [(x_hbm, x_ref), (w_hbm.at[0], w_ref), (cot_hbm, cot_ref), (wo_hbm, wo_ref)]
    x_load, w_load, cot_load, wo_load = fetch(pairs, sems)

    z, core, _, _ = place_of()
    pick = picker(1 - core)
    base = (z * 2 + core) * 4
    starts = (base - 4 + 8 * core, base, base + 4 - 8 * core)
    lane = lax.broadcasted_iota(jnp.int32, (4, 128), 1)
    slot = (lane & (BLOCK - 1)).astype(F32)
    table = lax.broadcasted_iota(jnp.int32, (1, 128), 1)
    listed, occupied = blocks_ref[0:4, :], blocks_ref[4:5, :].astype(F32)

    def limit(block):
        hit = jnp.max(jnp.where(listed == block, 1.0, 0.0), axis=1, keepdims=True)
        return hit * jnp.sum(jnp.where(table == block, occupied, 0.0), axis=1, keepdims=True)

    for w in range(0, 12, 2):
        block = starts[w // 4] + w % 4
        edge = jnp.where(lane < BLOCK, limit(block), limit(block + 1))
        bias_ref[:, w * BLOCK : (w + 2) * BLOCK] = jnp.where(slot < edge, 0.0, -1e30)

    x_load.wait()
    w_load.wait()
    q_ref[...] = nn(x_ref[...], w_ref[...]).astype(BF)
    cot_load.wait()
    wo_load.wait()
    u_ref[...] = nt(cot_ref[...], wo_ref[...]).astype(BF)
    pick_rows(pick, x_ref, cot_ref, xc_ref)


def mine_kernel(x_ref, cot_ref, xc_ref):
    pick_rows(picker(place_of()[1]), x_ref, cot_ref, xc_ref)


def attention_kernel(q_ref, u_ref, mate_ref, own_ref, far_ref, bias_ref, acts_ref, gf_ref, go_ref):
    factor = HD**-0.5
    window = (far_ref, own_ref, mate_ref)
    grads = (gf_ref, go_ref, acts_ref.at[2:4])
    lane = lax.broadcasted_iota(jnp.int32, (1, 128), 1)
    picks = [(lane < HD).astype(F32).astype(BF), (lane >= HD).astype(F32).astype(BF)]
    first = lax.broadcasted_iota(jnp.int32, (ROWS, 128), 1) < HD
    bias = [
        jnp.concatenate(
            [
                jnp.broadcast_to(bias_ref[b : b + 1, c * ROWS : (c + 1) * ROWS], (BLOCK, ROWS))
                for b in range(ROWS // BLOCK)
            ],
            axis=0,
        )
        for c in range(3)
    ]
    for pair in range(WIDTH // 128):
        cols = slice(pair * 128, (pair + 1) * 128)
        q2, u2 = q_ref[:, cols], u_ref[:, cols]
        q_turned, u_turned = q2.T, u2.T
        keys = [w[0, :, cols] for w in window]
        values = [w[1, :, cols] for w in window]
        key_parts, value_parts = [[], [], []], [[], [], []]
        att, dq = [], []
        for h, pick in enumerate(picks):
            rows = slice(h * HD, (h + 1) * HD)
            qm, um = q2 * pick, u2 * pick
            weights = [jnp.exp2(nt(qm, keys[c]) * (factor * LOG2E) + bias[c]) for c in range(3)]
            total = sum(jnp.sum(w, axis=1, keepdims=True) for w in weights)
            share = 1.0 / total
            probs = [w * share for w in weights]
            low = [p.astype(BF) for p in probs]
            dprob = [nt(um, values[c]) for c in range(3)]
            spread = sum(jnp.sum(p * d, axis=1, keepdims=True) for p, d in zip(probs, dprob))
            dscore = [(p * (d - spread) * factor).astype(BF) for p, d in zip(probs, dprob)]
            att.append(sum(nn(low[c], values[c]) for c in range(3)))
            dq.append(sum(nn(dscore[c], keys[c]) for c in range(3)))
            for c in range(3):
                key_parts[c].append(nn(q_turned[rows], dscore[c]))
                value_parts[c].append(nn(u_turned[rows], low[c]))
        acts_ref[0, :, cols] = jnp.where(first, att[0], att[1]).astype(BF)
        acts_ref[1, :, cols] = jnp.where(first, dq[0], dq[1]).astype(BF)
        for c in range(3):
            grads[c][0, :, cols] = jnp.concatenate(key_parts[c], axis=0).T.astype(grads[c].dtype)
            grads[c][1, :, cols] = jnp.concatenate(value_parts[c], axis=0).T.astype(grads[c].dtype)


def head_kernel(acts_ref, dkv_ref, wo_ref, w_ref, *outs, parts):
    head = place_of()[3]
    for to, k in zip(outs, parts):
        span = pl.ds(pl.multiple_of((head ^ k) * WIDTH, WIDTH), WIDTH)
        out = nn(acts_ref[0], wo_ref[:, span])
        grad = nt(acts_ref[1], w_ref[0, span, :])
        grad = grad + nt(dkv_ref[0], w_ref[1, span, :])
        grad = grad + nt(dkv_ref[1], w_ref[2, span, :])
        to[0] = out.astype(to.dtype)
        to[1] = grad.astype(to.dtype)


def head_sum_kernel(own_ref, r1_ref, r2_ref, r3_ref, x_ref, cot_ref, out_ref, grad_ref, token_ref):
    token_ref[...] = jnp.zeros_like(token_ref)
    span = pl.ds(pl.multiple_of(place_of()[3] * WIDTH, WIDTH), WIDTH)
    for i, (base, to) in enumerate(((x_ref, out_ref), (cot_ref, grad_ref))):
        total = own_ref[i] + r1_ref[i].astype(F32) + r2_ref[i].astype(F32) + r3_ref[i].astype(F32)
        to[...] = (base[:, span].astype(F32) + total).astype(BF)


def dkv_kernel(own_ref, a_ref, b_ref, out_ref):
    out_ref[...] = (own_ref[...] + a_ref[...].astype(F32) + b_ref[2:4].astype(F32)).astype(BF)


def early_kernel(mine_ref, other_ref, left_ref, right_ref, own_ref, rest_ref):
    for i, (side, act) in enumerate(((0, 1), (1, 0))):
        cols = slice(i * WIDTH, (i + 1) * WIDTH)
        g = nn(mine_ref[side], left_ref[act]) + nn(other_ref[side], right_ref[act])
        own_ref[:, cols] = g[:128]
        rest_ref[:, cols] = g[128:].astype(BF)


def late_kernel(mine_ref, other_ref, left_ref, right_ref, own1_ref, rest1_ref, own_ref, *sent):
    own_ref[:, : 2 * WIDTH] = own1_ref[...]
    for k in range(3):
        sent[k][:, : 2 * WIDTH] = rest1_ref[k * 128 : (k + 1) * 128, :]
    for i in range(2):
        cols = slice((2 + i) * WIDTH, (3 + i) * WIDTH)
        g = nn(mine_ref[0], left_ref[i]) + nn(other_ref[0], right_ref[i])
        own_ref[:, cols] = g[:128]
        for k in range(3):
            sent[k][:, cols] = g[(k + 1) * 128 : (k + 2) * 128].astype(BF)


def ysum_kernel(own_ref, r1_ref, r2_ref, r3_ref, kept_ref, *sent):
    total = own_ref[...]
    for r in (r1_ref, r2_ref, r3_ref):
        total = total + r[...].astype(F32)
    kept_ref[...] = total[:32]
    for m in range(3):
        sent[m][...] = total[32 * m + 32 : 32 * m + 64].astype(BF)


def sum_kernel(*refs):
    *parts, out_ref = refs
    total = parts[0][...].astype(F32)
    for r in parts[1:]:
        total = total + r[...].astype(F32)
    out_ref[...] = total.astype(BF)


def join_kernel(*refs, order):
    *parts, out_ref = refs
    rows = parts[0].shape[0]
    for i, r in zip(order, parts):
        out_ref[i * rows : (i + 1) * rows, :] = r[...]


def place_kernel(*refs):
    mine, other, (qkv_ref, out_ref, held, turned, sems) = refs[:4], refs[4:8], refs[8:]
    z, core, y, _ = place_of()
    copies = []
    for n, k in enumerate(PLACE_ORDER):
        block = pl.ds(pl.multiple_of((y ^ k) * 256, 256), 256)
        for array, column in ((0, 0), (1, 2), (2, 3), (3, 1)):
            cols = slice(column * WIDTH, (column + 1) * WIDTH)
            for side, blocks in ((core, mine), (1 - core, other)):
                for m in range(4):
                    rows = pl.ds(pl.multiple_of(side * 128 + ((z & 3) ^ m) * 32, 32), 32)
                    held[k, array, rows, :] = blocks[n][m * 32 : m * 32 + 32, cols].astype(F32)
            if array == 3:
                turned[k] = held[k, 3].T
                copy = pltpu.make_async_copy(turned.at[k], out_ref.at[:, block], sems.at[k, 3])
            else:
                copy = pltpu.make_async_copy(
                    held.at[k, array], qkv_ref.at[array, block], sems.at[k, array]
                )
            copy.start()
            copies.append(copy)
    for copy in copies:
        copy.wait()


def per_device(tokens, neighbours, counts, w_qkv, w_out, cotangent):
    x, listed, occupied, cot = tokens[0], neighbours[0], counts[0], cotangent[0]
    n = 16
    swap = [(i, i ^ 1) for i in range(n)]
    cross = [(i, (i + 1) % n if i % 2 else (i - 1) % n) for i in range(n)]

    def pair_z(k):
        return [(i, i ^ (2 * k)) for i in range(n)]

    def pair(k):
        return [(i, i ^ k) for i in range(4)]

    def swapped(a):
        return lax.ppermute(a, "spatial", swap)

    kv = call(
        kv_kernel,
        [shape((2, ROWS, WIDTH), BF)],
        [x, w_qkv],
        4 * ROWS * D * WIDTH,
        [HBM] * 2,
        scratch=[
            pltpu.VMEM((ROWS, D), BF),
            pltpu.VMEM((2, D, WIDTH), BF),
            pltpu.SemaphoreType.DMA((3,)),
        ],
        vmem=53.5,
    )[0]
    blocks = jnp.concatenate(
        [
            jnp.pad(listed, ((0, 0), (0, 128 - listed.shape[1])), constant_values=-1),
            jnp.pad(occupied[None], ((0, 0), (0, 128 - occupied.shape[0]))),
        ],
        axis=0,
    )
    q, u, xc_sent, bias = call(
        prep_kernel,
        [shape((ROWS, WIDTH), BF)] * 2 + [shape((2, 512, ROWS), BF), shape((4, 12 * BLOCK), F32)],
        [x, w_qkv, w_out, cot, blocks],
        8 * ROWS * D * WIDTH,
        [HBM] * 4 + [VMEM],
        scratch=[
            pltpu.VMEM((ROWS, D), BF),
            pltpu.VMEM((D, WIDTH), BF),
            pltpu.VMEM((WIDTH, D), BF),
            pltpu.VMEM((ROWS, D), BF),
            pltpu.SemaphoreType.DMA((4,)),
        ],
        vmem=53,
        after=[kv],
    )
    mate_kv = swapped(kv)
    far_kv = lax.ppermute(kv, "spatial", cross)

    xc_other = swapped(xc_sent)

    acts, grad_far, grad_own = call(
        attention_kernel,
        [
            shape((4, ROWS, WIDTH), BF),
            shape((2, ROWS, WIDTH), BF),
            shape((2, ROWS, WIDTH), F32),
        ],
        [q, u, mate_kv, kv, far_kv, bias],
        10 * 256 * 768 * 256,
        vmem=32,
    )
    from_far = lax.ppermute(grad_far, "spatial", cross)
    acts_other = swapped(acts)
    xc_mine = call(
        mine_kernel,
        [shape((2, 512, ROWS), BF)],
        [x, cot],
        4 * 512 * 256 * D,
        after=[acts],
    )[0]
    early = call(
        early_kernel,
        [shape((128, 512), F32), shape((384, 512), BF)],
        [xc_mine, xc_other, acts, acts_other],
        4 * 512 * 512 * 256,
    )
    dkv = call(
        dkv_kernel,
        [shape((2, ROWS, WIDTH), BF)],
        [grad_own, from_far, acts_other],
        2**18,
        after=[early[0]],
    )[0]
    own, *to_y = call(
        late_kernel,
        [shape((128, D), F32)] + [shape((128, D), BF)] * 3,
        [xc_mine, xc_other, dkv, swapped(dkv), *early],
        4 * 512 * 512 * 256,
    )
    from_y = [lax.ppermute(to_y[k - 1], "dp", pair(k)) for k in (1, 3, 2)]

    head_own, *to_head = call(
        functools.partial(head_kernel, parts=(0, 1, 3)),
        [shape((2, ROWS, WIDTH), F32)] + [shape((2, ROWS, WIDTH), BF)] * 2,
        [acts, dkv, w_out, w_qkv],
        6 * ROWS * WIDTH * D,
        after=[own],
    )
    from_head = [lax.ppermute(a, "head", pair(k)) for k, a in zip((1, 3), to_head)]

    own, *to_z = call(
        ysum_kernel,
        [shape((32, D), F32)] + [shape((32, D), BF)] * 3,
        [own] + from_y,
        2**20,
    )
    from_z = [lax.ppermute(to_z[m - 1], "spatial", pair_z(m)) for m in (2, 3, 1)]
    part = call(sum_kernel, [shape((32, D), BF)], [own] + from_z, 2**18)[0]
    far_part = lax.ppermute(part, "spatial", pair_z(4))
    chunk = call(sum_kernel, [shape((32, D), BF)], [part, far_part], 2**16)[0]
    pieces = [chunk] + [lax.ppermute(chunk, "spatial", pair_z(m)) for m in (1, 3, 2)]
    column = call(
        functools.partial(join_kernel, order=(0, 1, 3, 2)),
        [shape((128, D), BF)],
        pieces,
        2**16,
        after=from_head,
    )[0]
    mine = [column] + [lax.ppermute(column, "dp", pair(k)) for k in PLACE_ORDER[1:]]
    last = call(
        functools.partial(head_kernel, parts=(2,)),
        [shape((2, ROWS, WIDTH), BF)],
        [acts, dkv, w_out, w_qkv],
        2 * ROWS * WIDTH * D,
        after=[column],
    )[0]
    from_head.append(lax.ppermute(last, "head", pair(2)))
    layer_out, grad_tokens, token = call(
        head_sum_kernel,
        [shape((ROWS, WIDTH), BF)] * 2 + [shape((8, 128), F32)],
        [head_own, *from_head, x, cot],
        2**20,
    )
    other = [swapped(a) for a in mine]
    grad_qkv, grad_out = call(
        place_kernel,
        [shape((3, D, WIDTH), F32), shape((WIDTH, D), F32)],
        mine + other,
        2**20,
        scratch=[
            pltpu.VMEM((4, 4, 256, WIDTH), F32),
            pltpu.VMEM((4, WIDTH, 256), F32),
            pltpu.SemaphoreType.DMA((4, 4)),
        ],
        out_specs=[ANY, ANY],
        after=[token],
    )
    return layer_out[None], grad_tokens[None], grad_qkv, grad_out


def solution(mesh):
    in_specs = (
        P("dp", "spatial", None),
        P("dp", "spatial", None),
        P("dp", None),
        P(None, None, "head"),
        P("head", None),
        P("dp", "spatial", None),
    )
    out_specs = (
        P("dp", "spatial", "head"),
        P("dp", "spatial", "head"),
        P(None, None, "head"),
        P("head", None),
    )
    return jax.shard_map(
        per_device, mesh=mesh, in_specs=in_specs, out_specs=out_specs, check_vma=False
    )
```

```python
import functools

import jax
import jax.numpy as jnp
from jax import lax
from jax.experimental import pallas as pl
from jax.experimental.pallas import tpu as pltpu
from jax.sharding import PartitionSpec as P

HD = 64
BLOCK = 64
ROWS = 256
WIDTH = 256
D = 1024
PLACE_ORDER = (0, 2, 3, 1)
LOG2E = 1.4426950408889634
BF = jnp.bfloat16
F32 = jnp.float32
VMEM = pl.BlockSpec(memory_space=pltpu.VMEM)
ANY = pl.BlockSpec(memory_space=pl.ANY)
HBM = pl.BlockSpec(memory_space=pltpu.HBM)


def call(kernel, outs, operands, flops, in_specs=None, scratch=(), vmem=24, after=(), out_specs=None):
    moved = sum(a.size * a.dtype.itemsize for a in operands)
    moved += sum(o.size * o.dtype.itemsize for o in outs)
    count = len(operands)

    def body(*refs):
        kernel(*refs[:count], *refs[count + len(after) :])

    return pl.pallas_call(
        body,
        out_shape=outs,
        in_specs=(in_specs or [VMEM] * count) + [ANY] * len(after),
        out_specs=out_specs or [VMEM] * len(outs),
        scratch_shapes=list(scratch),
        compiler_params=pltpu.CompilerParams(vmem_limit_bytes=int(vmem * 2**20)),
        cost_estimate=pl.CostEstimate(flops=flops, bytes_accessed=moved, transcendentals=0),
    )(*operands, *after)


def shape(dims, kind):
    return jax.ShapeDtypeStruct(dims, kind)


def nn(a, b):
    return lax.dot_general(a, b, (((1,), (0,)), ((), ())), preferred_element_type=F32)


def nt(a, b):
    return lax.dot_general(a, b, (((1,), (1,)), ((), ())), preferred_element_type=F32)


def place_of():
    spatial = lax.axis_index("spatial")
    return spatial >> 1, spatial & 1, lax.axis_index("dp"), lax.axis_index("head")


def picker(side):
    z, _, y, _ = place_of()
    c = lax.broadcasted_iota(jnp.int32, (512, 1), 0)
    k, m = c >> 7, (c >> 5) & 3
    row = (y ^ k) * 256 + side * 128 + ((z & 3) ^ m) * 32 + (c & 31)
    feature = lax.broadcasted_iota(jnp.int32, (512, D), 1)
    return (feature == row).astype(F32).astype(BF)


def pick_rows(side, x_ref, cot_ref, out_ref):
    pick = picker(side)
    out_ref[0] = nt(pick, x_ref[...]).astype(BF)
    out_ref[1] = nt(pick, cot_ref[...]).astype(BF)


def fetch(pairs, sems):
    loads = [pltpu.make_async_copy(a, b, sems.at[i]) for i, (a, b) in enumerate(pairs)]
    for load in loads:
        load.start()
    return loads


def kv_kernel(x_hbm, w_hbm, out_ref, x_ref, w_ref, sems):
    pairs = [(x_hbm, x_ref), (w_hbm.at[1], w_ref.at[0]), (w_hbm.at[2], w_ref.at[1])]
    x_load, *loads = fetch(pairs, sems)
    x_load.wait()
    for i in range(2):
        loads[i].wait()
        out_ref[i] = nn(x_ref[...], w_ref[i]).astype(BF)


def prep_kernel(
    x_hbm, w_hbm, wo_hbm, cot_hbm, blocks_ref,
    q_ref, u_ref, xc_ref, bias_ref, x_ref, w_ref, wo_ref, cot_ref, sems
):
    pairs = [(x_hbm, x_ref), (w_hbm.at[0], w_ref), (cot_hbm, cot_ref), (wo_hbm, wo_ref)]
    x_load, w_load, cot_load, wo_load = fetch(pairs, sems)

    z, core, _, _ = place_of()
    base = (z * 2 + core) * 4
    starts = (base - 4 + 8 * core, base, base + 4 - 8 * core)
    lane = lax.broadcasted_iota(jnp.int32, (4, 128), 1)
    slot = (lane & (BLOCK - 1)).astype(F32)
    table = lax.broadcasted_iota(jnp.int32, (1, 128), 1)
    listed, occupied = blocks_ref[0:4, :], blocks_ref[4:5, :].astype(F32)

    def limit(block):
        hit = jnp.max(jnp.where(listed == block, 1.0, 0.0), axis=1, keepdims=True)
        return hit * jnp.sum(jnp.where(table == block, occupied, 0.0), axis=1, keepdims=True)

    for w in range(0, 12, 2):
        block = starts[w // 4] + w % 4
        edge = jnp.where(lane < BLOCK, limit(block), limit(block + 1))
        bias_ref[:, w * BLOCK : (w + 2) * BLOCK] = jnp.where(slot < edge, 0.0, -1e30)

    x_load.wait()
    w_load.wait()
    q_ref[...] = nn(x_ref[...], w_ref[...]).astype(BF)
    cot_load.wait()
    wo_load.wait()
    u_ref[...] = nt(cot_ref[...], wo_ref[...]).astype(BF)
    pick_rows(1 - core, x_ref, cot_ref, xc_ref)


def mine_kernel(x_ref, cot_ref, xc_ref):
    pick_rows(place_of()[1], x_ref, cot_ref, xc_ref)


def attention_kernel(q_ref, u_ref, mate_ref, own_ref, far_ref, bias_ref, acts_ref, gf_ref, go_ref):
    factor = HD**-0.5
    window = (far_ref, own_ref, mate_ref)
    grads = (gf_ref, go_ref, acts_ref.at[2:4])
    lane = lax.broadcasted_iota(jnp.int32, (1, 128), 1)
    picks = [(lane < HD).astype(F32).astype(BF), (lane >= HD).astype(F32).astype(BF)]
    first = lax.broadcasted_iota(jnp.int32, (ROWS, 128), 1) < HD
    bias = [
        jnp.concatenate(
            [
                jnp.broadcast_to(bias_ref[b : b + 1, c * ROWS : (c + 1) * ROWS], (BLOCK, ROWS))
                for b in range(ROWS // BLOCK)
            ],
            axis=0,
        )
        for c in range(3)
    ]
    for pair in range(WIDTH // 128):
        cols = slice(pair * 128, (pair + 1) * 128)
        q2, u2 = q_ref[:, cols], u_ref[:, cols]
        q_turned, u_turned = q2.T, u2.T
        keys = [w[0, :, cols] for w in window]
        values = [w[1, :, cols] for w in window]
        key_parts, value_parts = [[], [], []], [[], [], []]
        att, dq = [], []
        for h, pick in enumerate(picks):
            rows = slice(h * HD, (h + 1) * HD)
            qm, um = q2 * pick, u2 * pick
            weights = [jnp.exp2(nt(qm, keys[c]) * (factor * LOG2E) + bias[c]) for c in range(3)]
            total = sum(jnp.sum(w, axis=1, keepdims=True) for w in weights)
            share = 1.0 / total
            probs = [w * share for w in weights]
            low = [p.astype(BF) for p in probs]
            dprob = [nt(um, values[c]) for c in range(3)]
            spread = sum(jnp.sum(p * d, axis=1, keepdims=True) for p, d in zip(probs, dprob))
            dscore = [(p * (d - spread) * factor).astype(BF) for p, d in zip(probs, dprob)]
            att.append(sum(nn(low[c], values[c]) for c in range(3)))
            dq.append(sum(nn(dscore[c], keys[c]) for c in range(3)))
            for c in range(3):
                key_parts[c].append(nn(q_turned[rows], dscore[c]))
                value_parts[c].append(nn(u_turned[rows], low[c]))
        acts_ref[0, :, cols] = jnp.where(first, att[0], att[1]).astype(BF)
        acts_ref[1, :, cols] = jnp.where(first, dq[0], dq[1]).astype(BF)
        for c in range(3):
            grads[c][0, :, cols] = jnp.concatenate(key_parts[c], axis=0).T.astype(grads[c].dtype)
            grads[c][1, :, cols] = jnp.concatenate(value_parts[c], axis=0).T.astype(grads[c].dtype)


def head_kernel(acts_ref, dkv_ref, wo_ref, w_ref, *outs, parts):
    head = place_of()[3]
    for to, k in zip(outs, parts):
        span = pl.ds(pl.multiple_of((head ^ k) * WIDTH, WIDTH), WIDTH)
        out = nn(acts_ref[0], wo_ref[:, span])
        grad = nt(acts_ref[1], w_ref[0, span, :])
        grad = grad + nt(dkv_ref[0], w_ref[1, span, :])
        grad = grad + nt(dkv_ref[1], w_ref[2, span, :])
        to[0] = out.astype(to.dtype)
        to[1] = grad.astype(to.dtype)


def head_sum_kernel(own_ref, r1_ref, r2_ref, r3_ref, x_ref, cot_ref, out_ref, grad_ref, token_ref):
    token_ref[...] = jnp.zeros_like(token_ref)
    span = pl.ds(pl.multiple_of(place_of()[3] * WIDTH, WIDTH), WIDTH)
    for i, (base, to) in enumerate(((x_ref, out_ref), (cot_ref, grad_ref))):
        total = own_ref[i] + r1_ref[i].astype(F32) + r2_ref[i].astype(F32) + r3_ref[i].astype(F32)
        to[...] = (base[:, span].astype(F32) + total).astype(BF)


def dkv_kernel(own_ref, a_ref, b_ref, out_ref):
    out_ref[...] = (own_ref[...] + a_ref[...].astype(F32) + b_ref[2:4].astype(F32)).astype(BF)


def early_kernel(mine_ref, other_ref, left_ref, right_ref, own_ref, rest_ref):
    for i, (side, act) in enumerate(((0, 1), (1, 0))):
        cols = slice(i * WIDTH, (i + 1) * WIDTH)
        g = nn(mine_ref[side], left_ref[act]) + nn(other_ref[side], right_ref[act])
        own_ref[:, cols] = g[:128]
        rest_ref[:, cols] = g[128:].astype(BF)


def late_kernel(mine_ref, other_ref, left_ref, right_ref, own1_ref, rest1_ref, own_ref, *sent):
    own_ref[:, : 2 * WIDTH] = own1_ref[...]
    for k in range(3):
        sent[k][:, : 2 * WIDTH] = rest1_ref[k * 128 : (k + 1) * 128, :]
    for i in range(2):
        cols = slice((2 + i) * WIDTH, (3 + i) * WIDTH)
        g = nn(mine_ref[0], left_ref[i]) + nn(other_ref[0], right_ref[i])
        own_ref[:, cols] = g[:128]
        for k in range(3):
            sent[k][:, cols] = g[(k + 1) * 128 : (k + 2) * 128].astype(BF)


def ysum_kernel(own_ref, r1_ref, r2_ref, r3_ref, kept_ref, *sent):
    total = own_ref[...]
    for r in (r1_ref, r2_ref, r3_ref):
        total = total + r[...].astype(F32)
    kept_ref[...] = total[:32]
    for m in range(3):
        sent[m][...] = total[32 * m + 32 : 32 * m + 64].astype(BF)


def sum_kernel(*refs):
    *parts, out_ref = refs
    total = parts[0][...].astype(F32)
    for r in parts[1:]:
        total = total + r[...].astype(F32)
    out_ref[...] = total.astype(BF)


def join_kernel(*refs, order):
    *parts, out_ref = refs
    rows = parts[0].shape[0]
    for i, r in zip(order, parts):
        out_ref[i * rows : (i + 1) * rows, :] = r[...]


def place_kernel(*refs):
    mine, other, (qkv_ref, out_ref, held, turned, sems) = refs[:4], refs[4:8], refs[8:]
    z, core, y, _ = place_of()
    copies = []
    for n, k in enumerate(PLACE_ORDER):
        block = pl.ds(pl.multiple_of((y ^ k) * 256, 256), 256)
        for array, column in ((3, 1), (0, 0), (1, 2), (2, 3)):
            cols = slice(column * WIDTH, (column + 1) * WIDTH)
            for side, blocks in ((core, mine), (1 - core, other)):
                for m in range(4):
                    rows = pl.ds(pl.multiple_of(side * 128 + ((z & 3) ^ m) * 32, 32), 32)
                    held[k, array, rows, :] = blocks[n][m * 32 : m * 32 + 32, cols].astype(F32)
            if array == 3:
                turned[k] = held[k, 3].T
                copy = pltpu.make_async_copy(turned.at[k], out_ref.at[:, block], sems.at[k, 3])
            else:
                copy = pltpu.make_async_copy(
                    held.at[k, array], qkv_ref.at[array, block], sems.at[k, array]
                )
            copy.start()
            copies.append(copy)
    for copy in copies:
        copy.wait()


def per_device(tokens, neighbours, counts, w_qkv, w_out, cotangent):
    x, listed, occupied, cot = tokens[0], neighbours[0], counts[0], cotangent[0]
    n = 16
    swap = [(i, i ^ 1) for i in range(n)]
    cross = [(i, (i + 1) % n if i % 2 else (i - 1) % n) for i in range(n)]

    def pair_z(k):
        return [(i, i ^ (2 * k)) for i in range(n)]

    def pair(k):
        return [(i, i ^ k) for i in range(4)]

    def swapped(a):
        return lax.ppermute(a, "spatial", swap)

    kv = call(
        kv_kernel,
        [shape((2, ROWS, WIDTH), BF)],
        [x, w_qkv],
        4 * ROWS * D * WIDTH,
        [HBM] * 2,
        scratch=[
            pltpu.VMEM((ROWS, D), BF),
            pltpu.VMEM((2, D, WIDTH), BF),
            pltpu.SemaphoreType.DMA((3,)),
        ],
        vmem=53.5,
    )[0]
    blocks = jnp.concatenate(
        [
            jnp.pad(listed, ((0, 0), (0, 128 - listed.shape[1])), constant_values=-1),
            jnp.pad(occupied[None], ((0, 0), (0, 128 - occupied.shape[0]))),
        ],
        axis=0,
    )
    q, u, xc_sent, bias = call(
        prep_kernel,
        [shape((ROWS, WIDTH), BF)] * 2 + [shape((2, 512, ROWS), BF), shape((4, 12 * BLOCK), F32)],
        [x, w_qkv, w_out, cot, blocks],
        8 * ROWS * D * WIDTH,
        [HBM] * 4 + [VMEM],
        scratch=[
            pltpu.VMEM((ROWS, D), BF),
            pltpu.VMEM((D, WIDTH), BF),
            pltpu.VMEM((WIDTH, D), BF),
            pltpu.VMEM((ROWS, D), BF),
            pltpu.SemaphoreType.DMA((4,)),
        ],
        vmem=53,
        after=[kv],
    )
    mate_kv = swapped(kv)
    far_kv = lax.ppermute(kv, "spatial", cross)

    xc_other = swapped(xc_sent)

    acts, grad_far, grad_own = call(
        attention_kernel,
        [
            shape((4, ROWS, WIDTH), BF),
            shape((2, ROWS, WIDTH), BF),
            shape((2, ROWS, WIDTH), F32),
        ],
        [q, u, mate_kv, kv, far_kv, bias],
        10 * 256 * 768 * 256,
        vmem=32,
    )
    from_far = lax.ppermute(grad_far, "spatial", cross)
    acts_other = swapped(acts)
    xc_mine = call(
        mine_kernel,
        [shape((2, 512, ROWS), BF)],
        [x, cot],
        4 * 512 * 256 * D,
        after=[acts],
    )[0]
    early = call(
        early_kernel,
        [shape((128, 512), F32), shape((384, 512), BF)],
        [xc_mine, xc_other, acts, acts_other],
        4 * 512 * 512 * 256,
    )
    dkv = call(
        dkv_kernel,
        [shape((2, ROWS, WIDTH), BF)],
        [grad_own, from_far, acts_other],
        2**18,
        after=[early[0]],
    )[0]
    own, *to_y = call(
        late_kernel,
        [shape((128, D), F32)] + [shape((128, D), BF)] * 3,
        [xc_mine, xc_other, dkv, swapped(dkv), *early],
        4 * 512 * 512 * 256,
    )
    from_y = [lax.ppermute(to_y[k - 1], "dp", pair(k)) for k in (1, 3, 2)]

    head_own, *to_head = call(
        functools.partial(head_kernel, parts=(0, 1, 3, 2)),
        [shape((2, ROWS, WIDTH), F32)] + [shape((2, ROWS, WIDTH), BF)] * 3,
        [acts, dkv, w_out, w_qkv],
        8 * ROWS * WIDTH * D,
        after=[own],
    )
    from_head = [lax.ppermute(a, "head", pair(k)) for k, a in zip((1, 3, 2), to_head)]

    own, *to_z = call(
        ysum_kernel,
        [shape((32, D), F32)] + [shape((32, D), BF)] * 3,
        [own] + from_y,
        2**20,
        after=from_head[:2],
    )
    from_z = [lax.ppermute(to_z[m - 1], "spatial", pair_z(m)) for m in (2, 3, 1)]
    part = call(sum_kernel, [shape((32, D), BF)], [own] + from_z, 2**18, after=from_head[2:])[0]
    far_part = lax.ppermute(part, "spatial", pair_z(4))
    chunk = call(sum_kernel, [shape((32, D), BF)], [part, far_part], 2**16)[0]
    pieces = [chunk] + [lax.ppermute(chunk, "spatial", pair_z(m)) for m in (1, 3, 2)]
    column = call(
        functools.partial(join_kernel, order=(0, 1, 3, 2)),
        [shape((128, D), BF)],
        pieces,
        2**16,
    )[0]
    mine = [column] + [lax.ppermute(column, "dp", pair(k)) for k in PLACE_ORDER[1:]]
    layer_out, grad_tokens, token = call(
        head_sum_kernel,
        [shape((ROWS, WIDTH), BF)] * 2 + [shape((8, 128), F32)],
        [head_own, *from_head, x, cot],
        2**20,
    )
    other = [swapped(a) for a in mine]
    grad_qkv, grad_out = call(
        place_kernel,
        [shape((3, D, WIDTH), F32), shape((WIDTH, D), F32)],
        mine + other,
        2**20,
        scratch=[
            pltpu.VMEM((4, 4, 256, WIDTH), F32),
            pltpu.VMEM((4, WIDTH, 256), F32),
            pltpu.SemaphoreType.DMA((4, 4)),
        ],
        out_specs=[ANY, ANY],
        after=[token],
    )
    return layer_out[None], grad_tokens[None], grad_qkv, grad_out


def solution(mesh):
    in_specs = (
        P("dp", "spatial", None),
        P("dp", "spatial", None),
        P("dp", None),
        P(None, None, "head"),
        P("head", None),
        P("dp", "spatial", None),
    )
    out_specs = (
        P("dp", "spatial", "head"),
        P("dp", "spatial", "head"),
        P(None, None, "head"),
        P("head", None),
    )
    return jax.shard_map(
        per_device, mesh=mesh, in_specs=in_specs, out_specs=out_specs, check_vma=False
    )
```
